256 devices in a mesh: dp: 32 (over z, x), vocab: 8 (over y, core).
Axes of the slice: x: 4, y: 4, z: 8, core: 2. Of those that a mesh axis runs over, the one named last changes fastest.
Arguments:
- hidden: bfloat16 [256, 7168], P('dp'), may hold values from -12 to 12
- final_hidden: bfloat16 [256, 7168], P('dp'), may hold values from -12 to 12
- translator: bfloat16 [7168, 7168], P('dp', 'vocab'), may hold values from -0.0625 to 0.0625
- offset: float32 [7168], P('vocab'), may hold values from -3 to 3
- norm_gain: bfloat16 [7168], replicated, may hold values from 0.5 to 1.5
- unembed: bfloat16 [7168, 131072], P(None, ('dp', 'vocab')), may hold values from -1 to 1
Outputs:
- grad_translator: float32 [7168, 7168], P('dp', 'vocab')
- grad_offset: float32 [7168], P('vocab')
- divergence: float32 [256], P('dp')
The draws below stay inside these ranges and needn't reach their ends.
All inputs are finite; a program needn't handle non-finite values.
Results may differ from the reference program's by a relative error of at most 0.0063.
Values may be sent and summed in bfloat16 or wider, within the bound.
A program may use at most 128 MiB of HBM per device.

```python
import math
import jax
import jax.numpy as jnp
from jax import lax

D = 7168
TOKENS = 256
VOCAB = 131072


def sign_rows(key):
    coin_flips = jax.random.bernoulli(jax.random.fold_in(key, 11), 0.5, (8, D))
    return jnp.where(coin_flips, 1.0, -1.0).astype(jnp.float32)


def rough_columns(key, width, top):
    trend_line = jnp.exp(jnp.linspace(0.0, math.log(top), width))
    return trend_line * jnp.exp(jax.random.uniform(key, (width,), minval=math.log(0.6), maxval=math.log(1.6)))


def draw_hidden(key, part):
    patterns = sign_rows(key)
    key = jax.random.fold_in(key, 2)
    key_values, key_columns = jax.random.split(key, 2)
    values = jax.random.normal(key_values, (TOKENS, D), jnp.float32) * rough_columns(key_columns, D, 3.0)
    values = values.at[:8].set(2.0 * patterns)
    return jnp.clip(values, -12.0, 12.0).astype(jnp.bfloat16)


def draw_final_hidden(key, part):
    patterns = sign_rows(key)
    key = jax.random.fold_in(key, 5)
    key_values = jax.random.fold_in(key, 0)
    key_columns = jax.random.fold_in(key, 1)
    key_extra = jax.random.fold_in(key, 4)
    values = jax.random.normal(key_values, (TOKENS, D), jnp.float32) * rough_columns(key_columns, D, 3.0)
    extra_rows = 2.0 * patterns[4:8] + 2.04 * jax.random.normal(key_extra, (4, D), jnp.float32)
    values = values.at[:4].set(2.0 * patterns[:4])
    values = values.at[4:8].set(extra_rows)
    return jnp.clip(values, -12.0, 12.0).astype(jnp.bfloat16)


def draw_unembed(key, part):
    patterns = sign_rows(key)
    key = jax.random.fold_in(key, 7)
    key_values, key_columns, key_picks = jax.random.split(key, 3)
    spread = jnp.exp(jnp.linspace(math.log(0.3), math.log(1.5), VOCAB))
    spread = spread * jnp.exp(jax.random.uniform(key_columns, (VOCAB,), minval=math.log(0.7), maxval=math.log(1.4)))
    values = jax.random.normal(key_values, (D, VOCAB), jnp.float32) * spread * (1.0 / math.sqrt(D))
    band_width = VOCAB // 12
    chosen = jnp.arange(12, dtype=jnp.int32) * band_width + jax.random.randint(key_picks, (12,), 0, band_width)
    strength = jnp.array([130.0, 170.0, 210.0, 250.0], jnp.float32) / D
    first = patterns[:4] * strength[:, None]
    second = patterns[:4] * (strength[:, None] - 2.0 / D)
    paired = jnp.stack([first, second], axis=1).reshape(8, D)
    single_strength = jnp.array([13.5, 14.2, 14.9, 15.6], jnp.float32) / (0.7 * D)
    singles = patterns[4:8] * single_strength[:, None]
    columns = jnp.concatenate([paired, singles], axis=0)
    values = values.at[:, chosen].set(columns.T)
    return jnp.clip(values, -1.0, 1.0).astype(jnp.bfloat16)


def shard_levels(key, dims, pieces, low, largest):
    factor_of, own = 1.0, jax.random.fold_in(key, 6)
    for position, blocks in pieces:
        heights = jnp.exp(jax.random.uniform(jax.random.fold_in(own, position), (blocks,), jnp.float32, low / len(pieces), largest / len(pieces)))
        factor_of = factor_of * jnp.repeat(heights, dims[position] // blocks).reshape([-1 if axis == position else 1 for axis in range(len(dims))])
    return factor_of


def bell_draw(stream_key, shape, scale, limit, cuts=(), kind=jnp.bfloat16):
    drawn = scale * jax.random.normal(stream_key, shape, jnp.float32)
    if cuts:
        drawn = drawn * shard_levels(stream_key, shape, cuts, -0.22, 0.18)
    return jnp.clip(drawn, -limit, limit).astype(kind)


def setup_inputs(seed: int = 0) -> dict:
    splits = jax.random.split(jax.random.key(seed), 7)
    hidden = draw_hidden(jax.random.fold_in(splits[6], 71), 0)
    final_hidden = draw_final_hidden(jax.random.fold_in(splits[6], 71), 0)
    translator = bell_draw(splits[2], (D, D), D ** -0.5, 0.0625, ((0, 32), (1, 8)))
    offset = bell_draw(splits[3], (D,), 0.5, 3.0, ((0, 8),), jnp.float32)
    norm_gain = jnp.clip(1.0 + 0.1 * jax.random.normal(splits[4], (D,), jnp.float32), 0.5, 1.5).astype(jnp.bfloat16)
    unembed = draw_unembed(jax.random.fold_in(splits[6], 71), 0)
    return {"hidden": hidden, "final_hidden": final_hidden, "translator": translator, "offset": offset, "norm_gain": norm_gain, "unembed": unembed}


EPSILON = 1e-06

def reference(hidden, final_hidden, translator, offset, norm_gain, unembed):
    gain_all = norm_gain.astype(jnp.float32)
    lens_state = hidden.astype(jnp.float32) + jnp.dot(hidden, translator, preferred_element_type=jnp.float32) + offset
    inverse_rms = lax.rsqrt(lax.optimization_barrier(jnp.mean(lens_state * lens_state, axis=1, keepdims=True)) + EPSILON)
    lens_in = (lens_state * inverse_rms * gain_all).astype(jnp.bfloat16)
    final_all = final_hidden.astype(jnp.float32)
    final_inverse = lax.rsqrt(lax.optimization_barrier(jnp.mean(final_all * final_all, axis=1, keepdims=True)) + EPSILON)
    final_in = (final_all * final_inverse * gain_all).astype(jnp.bfloat16)
    lens_logits = jnp.dot(lens_in, unembed, preferred_element_type=jnp.float32)
    final_logits = jnp.dot(final_in, unembed, preferred_element_type=jnp.float32)
    lens_total = jax.nn.logsumexp(lens_logits, axis=1, keepdims=True)
    final_total = jax.nn.logsumexp(final_logits, axis=1, keepdims=True)
    target = jnp.exp(final_logits - final_total)
    predicted = jnp.exp(lens_logits - lens_total)
    divergence = lax.optimization_barrier(jnp.sum(target * (final_logits - final_total - lens_logits + lens_total), axis=1))
    logit_grad = (predicted - target).astype(jnp.bfloat16)
    state_grad = jnp.dot(logit_grad, unembed.T, preferred_element_type=jnp.float32)
    weighted = gain_all * state_grad
    slope_term = lax.optimization_barrier(jnp.mean(weighted * lens_state, axis=1, keepdims=True))
    state_delta = inverse_rms * weighted - lens_state * inverse_rms ** 3 * slope_term
    grad_translator = jnp.dot(hidden.T, state_delta.astype(jnp.bfloat16), preferred_element_type=jnp.float32)
    grad_offset = lax.optimization_barrier(jnp.sum(state_delta, axis=0))
    return (grad_translator, grad_offset, divergence)
```

```python
import functools

import jax
import jax.numpy as jnp
from jax import lax
from jax.experimental import pallas as pl
from jax.experimental.pallas import tpu as pltpu
from jax.sharding import PartitionSpec as P

MESH = pl.DeviceIdType.MESH
F32, BF16 = jnp.float32, jnp.bfloat16
D = 7168
COLS = 896
ROWS = 224
VOC = 512
EPSILON = 1e-06
NZ, NX, NY = 8, 4, 4


def pack(a):
    low = jnp.concatenate([a[:, 512:], jnp.zeros((8, 128), F32)], axis=1)
    return jnp.concatenate([a[:, :512], low], axis=0).astype(BF16)


def unpack(blocks):
    wide = blocks.astype(F32)
    return jnp.concatenate([wide[:, :8], wide[:, 8:, :384]], axis=2).reshape(64, COLS).astype(BF16)


def merge(tiles):
    lens_peak = functools.reduce(jnp.maximum, [t[0:1] for t in tiles])
    final_peak = functools.reduce(jnp.maximum, [t[2:3] for t in tiles])
    lens_sum = sum(t[1:2] * jnp.exp(t[0:1] - lens_peak) for t in tiles)
    scales = [jnp.exp(t[2:3] - final_peak) for t in tiles]
    final_sum = sum(t[3:4] * s for t, s in zip(tiles, scales))
    cross = sum(t[4:5] * s for t, s in zip(tiles, scales))
    return stack_rows([lens_peak, lens_sum, final_peak, final_sum, cross])


def stack_rows(rows):
    place = lax.broadcasted_iota(jnp.int32, (8, 256), 0)
    tile = jnp.zeros((8, 256), F32)
    for i, row in enumerate(rows):
        tile = jnp.where(place == i, jnp.broadcast_to(row, (8, 256)), tile)
    return tile


def kernel(
    hid, fin, tw, off, gain, unemb, gt, goff, div,
    u, hpack, ha, xsend, hx, rows_t, twp, mapped, cx, sx, dz,
    f_norm, f_pack, f_z, f_buf, l_pack, l_z, l_buf, l_state,
    v_send, v_recv, w_send, w_recv,
    l_log, f_log, st_core, st_y, st_x, st_z, cols, grad,
    c_send, c_recv, acc, ry0, rx1, r0, r1, rx0, ry1, sz, rz,
    sd_pack, sd_z, sd,
    u_sem, a_s, a_r, b_s, b_r, c_s, c_r, d_s, d_r, v_s, v_r, w_s, w_r,
    fz_s, fz_r, f1_s, f1_r, f2_s, f2_r, fc_s, fc_r,
    lz_s, lz_r, l1_s, l1_r, l2_s, l2_r, lc_s, lc_r,
    tc_s, tc_r, ty_s, ty_r, tx_s, tx_r, tz_s, tz_r,
    gc_s, gc_r, g1_s, g1_r, g2_s, g2_r, gz_s, gz_r,
    oz_s, oz_r, ox_s, ox_r,
):
    r, c = lax.axis_index("dp"), lax.axis_index("vocab")
    z, x = lax.div(r, NX), lax.rem(r, NX)
    y, k = lax.div(c, 2), lax.rem(c, 2)
    half, quarter = lax.div(z, 4), lax.rem(z, 4)
    feat = pl.ds(pl.multiple_of(c * COLS, 128), COLS)

    def at_z(i):
        return (i * NX + x, c)

    def at_x(i):
        return (z * NX + i, c)

    def at_y(i):
        return (r, i * 2 + k)

    sibling = (r, y * 2 + (1 - k))
    unsent = []

    def copy(src, dst, ss, rs, dev):
        return pltpu.make_async_remote_copy(
            src_ref=src, dst_ref=dst, send_sem=ss, recv_sem=rs, device_id=dev, device_id_type=MESH
        )

    def send(src, dst, ss, rs, dev):
        one = copy(src, dst, ss, rs, dev)
        one.start()
        unsent.append(one)

    def recv(land, ss, rs, dev):
        copy(land, land, ss, rs, dev).wait_recv()

    def others(n, me):
        return [(d - 1, lax.rem(me + d, n), lax.rem(me + (n - d), n)) for d in range(1, n)]

    barrier = pltpu.get_barrier_semaphore()
    partners = [at_z(t) for _, t, _ in others(NZ, z)] + [at_x(t) for _, t, _ in others(NX, x)]
    group = [(d - 1, (r, lax.rem(c + d, 8)), (r, lax.rem(c + (8 - d), 8))) for d in range(1, 8)]
    partners += [t for _, t, _ in group]
    for p in partners:
        pl.semaphore_signal(barrier, inc=1, device_id=p, device_id_type=MESH)
    load_u = pltpu.make_async_copy(unemb, u, u_sem)
    load_u.start()

    for i in range(NZ):
        hpack[i] = pack(hid[:, i * COLS : (i + 1) * COLS].astype(F32))
    wide = fin[...].astype(F32)
    final_inverse = lax.rsqrt(jnp.sum(wide * wide, axis=1, keepdims=True) / D + EPSILON)
    f_norm[...] = wide * final_inverse * gain[...].astype(F32)
    f_pack[...] = pack(f_norm[:, feat])
    twp[:ROWS] = tw[...]
    twp[ROWS:] = jnp.zeros((256 - ROWS, COLS), BF16)
    pl.semaphore_wait(barrier, len(partners))

    for j, t, _ in others(NZ, z):
        send(hpack.at[t], ha.at[z], a_s.at[j], a_r.at[j], at_z(t))
    for j, t, _ in others(NZ, z):
        send(f_pack, f_z.at[z], fz_s.at[j], fz_r.at[j], at_z(t))
    ha[z] = hpack[z]
    f_z[z] = f_pack[...]
    for j, _, s in others(NZ, z):
        recv(ha.at[s], a_s.at[j], a_r.at[j], at_z(s))
    flat = unpack(ha[...]).astype(F32)
    for i in range(NX):
        part = jnp.concatenate([flat[:, i * ROWS : (i + 1) * ROWS], jnp.zeros((64, 256 - ROWS), F32)], axis=1)
        xsend[i] = part.astype(BF16).reshape(2, 32, 256)
    for j, t, _ in others(NX, x):
        send(xsend.at[t], hx.at[:, x], b_s.at[j], b_r.at[j], at_x(t))
    hx[:, x] = xsend[x]


    def own_pieces(buf, zbuf, zs, zr, s1, r1, s2, r2, sc, rc, firsts):
        for j, _, s in others(NZ, z):
            recv(zbuf.at[s], zs.at[j], zr.at[j], at_z(s))
        flat = unpack(zbuf[...])
        for h in range(2):
            buf[k, y, h, x] = flat[h * 32 : (h + 1) * 32]
        for h, first in enumerate(firsts):
            piece = buf.at[k, y, h, x]
            ways = [(NX, x, at_x), (NY, y, at_y)]
            (n1, m1, at1), (n2, m2, at2) = ways if first == "x" else ways[::-1]
            for j, t, _ in others(n1, m1):
                send(piece, piece, s1.at[h, j], r1.at[h, j], at1(t))
            for j, t, _ in others(n2, m2):
                send(piece, piece, s2.at[h, 0, j], r2.at[h, 0, j], at2(t))
            send(piece, piece, sc.at[h, 0, 0], rc.at[h, 0, 0], sibling)

    def forward(buf, s1, r1, s2, r2, sc, rc, firsts):
        for q in range(1, 4):
            for h, first in enumerate(firsts):
                if first == "x":
                    s = lax.rem(x + (NX - q), NX)
                    piece, dev, n2, m2, at2 = buf.at[k, y, h, s], at_x(s), NY, y, at_y
                    slot = (h, 0, q)
                else:
                    s = lax.rem(y + (NY - q), NY)
                    piece, dev, n2, m2, at2 = buf.at[k, s, h, x], at_y(s), NX, x, at_x
                    slot = (h, q, 0)
                recv(piece, s1.at[h, q - 1], r1.at[h, q - 1], dev)
                for j, t, _ in others(n2, m2):
                    send(piece, piece, s2.at[h, q, j], r2.at[h, q, j], at2(t))
                send(piece, piece, sc.at[slot], rc.at[slot], sibling)

    def rest(buf, s2, r2, sc, rc, firsts, each=lambda q: None):
        for q in range(1, 4):
            for j in range(4):
                for h, first in enumerate(firsts):
                    if first == "x":
                        yy, xx = lax.rem(y + (NY - q), NY), lax.rem(x + (NX - j), NX)
                        dev, slot = at_y(yy), (h, q, j)
                    else:
                        yy, xx = lax.rem(y + (NY - j), NY), lax.rem(x + (NX - q), NX)
                        dev, slot = at_x(xx), (h, j, q)
                    piece = buf.at[k, yy, h, xx]
                    recv(piece, s2.at[h, j, q - 1], r2.at[h, j, q - 1], dev)
                    send(piece, piece, sc.at[slot], rc.at[slot], sibling)
            each(q)

    def logits(buf, log, kk, yy):
        block = pl.ds(pl.multiple_of((yy * 2 + kk) * COLS, 128), COLS)
        log[...] += jnp.dot(buf[kk, yy].reshape(256, COLS), u[block, :], preferred_element_type=F32)

    def own_logits(buf, log):
        def step(q, _):
            logits(buf, log, k, lax.rem(y + (NY - q), NY))
            return 0

        lax.fori_loop(0, NY, step, 0)

    def sibling_logits(buf, log, sc, rc):
        def step(q, _):
            yy = lax.rem(y + (NY - q), NY)
            for h in range(2):
                for j in range(4):
                    xx = lax.rem(x + (NX - j), NX)
                    recv(buf.at[1 - k, yy, h, xx], sc.at[h, q, j], rc.at[h, q, j], sibling)
            logits(buf, log, 1 - k, yy)
            return 0

        lax.fori_loop(0, NY, step, 0)

    f_first, l_first = ("x", "x"), ("x", "y")
    own_pieces(f_buf, f_z, fz_s, fz_r, f1_s, f1_r, f2_s, f2_r, fc_s, fc_r, f_first)

    for j, _, s in others(NX, x):
        recv(hx.at[:, s], b_s.at[j], b_r.at[j], at_x(s))
    rows = hx[...].reshape(256, 256)
    mapped[...] = jnp.dot(rows, twp[...], preferred_element_type=F32).reshape(2, NX, 32, COLS)
    for j, t, _ in others(NX, x):
        send(mapped.at[:, t], cx.at[j], c_s.at[j], c_r.at[j], at_x(t))
    rows_t[...] = rows.astype(F32).T.astype(BF16)
    forward(f_buf, f1_s, f1_r, f2_s, f2_r, fc_s, fc_r, f_first)
    l_log[...] = jnp.zeros_like(l_log)
    f_log[...] = jnp.zeros_like(f_log)
    for j, t, s in others(NX, x):
        recv(cx.at[j], c_s.at[j], c_r.at[j], at_x(s))
    sx[...] = (mapped[:, x] + cx[0] + cx[1] + cx[2]).reshape(NZ, 8, COLS)
    for j, t, _ in others(NZ, z):
        send(sx.at[t], dz.at[j], d_s.at[j], d_r.at[j], at_z(t))
    base = hid[:, feat].astype(F32) + off[...] + sx[z]
    gain_part = gain[:, feat].astype(F32)
    for j, _, s in others(NZ, z):
        recv(dz.at[j], d_s.at[j], d_r.at[j], at_z(s))
        base = base + dz[j]
    l_state[...] = base

    def group_sum(part, snd, rcv, ss, rs):
        snd[...] = jnp.broadcast_to(part, (8, 128))
        for j, t, _ in group:
            send(snd, rcv.at[j], ss.at[j], rs.at[j], t)
        total = snd[...]
        for j, _, s in group:
            recv(rcv.at[j], ss.at[j], rs.at[j], s)
            total = total + rcv[j]
        return total[:, 0:1]

    squares = group_sum(jnp.sum(base * base, axis=1, keepdims=True), v_send, v_recv, v_s, v_r)
    inverse = lax.rsqrt(squares / D + EPSILON)
    l_pack[...] = pack(l_state[...] * inverse * gain_part)
    for j, t, _ in others(NZ, z):
        send(l_pack, l_z.at[z], lz_s.at[j], lz_r.at[j], at_z(t))
    l_z[z] = l_pack[...]
    load_u.wait()
    rest(f_buf, f2_s, f2_r, fc_s, fc_r, f_first)
    own_pieces(l_buf, l_z, lz_s, lz_r, l1_s, l1_r, l2_s, l2_r, lc_s, lc_r, l_first)
    own_logits(f_buf, f_log)
    forward(l_buf, l1_s, l1_r, l2_s, l2_r, lc_s, lc_r, l_first)
    sibling_logits(f_buf, f_log, fc_s, fc_r)
    rest(l_buf, l2_s, l2_r, lc_s, lc_r, l_first)
    own_logits(l_buf, l_log)
    sibling_logits(l_buf, l_log, lc_s, lc_r)

    place = lax.broadcasted_iota(jnp.int32, (32, 128), 1)

    def local(i, _):
        part = pl.ds(pl.multiple_of(i * 32, 32), 32)
        a, b = l_log[part, :], f_log[part, :]
        a_peak, b_peak = jnp.max(a, axis=1, keepdims=True), jnp.max(b, axis=1, keepdims=True)
        weight = jnp.exp(b - b_peak)
        found = [
            a_peak, jnp.sum(jnp.exp(a - a_peak), axis=1, keepdims=True), b_peak,
            jnp.sum(weight, axis=1, keepdims=True), jnp.sum(weight * (b - a), axis=1, keepdims=True),
        ]
        tile = jnp.zeros((32, 128), F32)
        for n, v in enumerate(found):
            tile = jnp.where(place == n, jnp.broadcast_to(v, (32, 128)), tile)
        cols[part, :] = tile
        return 0

    lax.fori_loop(0, 8, local, 0)
    st_core[0] = cols[...].T[:8]
    send(st_core.at[0], st_core.at[1], tc_s, tc_r, sibling)
    recv(st_core.at[1], tc_s, tc_r, sibling)
    st_y[3] = merge([st_core[0], st_core[1]])
    for buf, n, me, at, ss, rs, nxt in (
        (st_y, NY, y, at_y, ty_s, ty_r, st_x),
        (st_x, NX, x, at_x, tx_s, tx_r, st_z),
        (st_z, NZ, z, at_z, tz_s, tz_r, None),
    ):
        for j, t, _ in others(n, me):
            send(buf.at[n - 1], buf.at[j], ss.at[j], rs.at[j], at(t))
        for j, _, s in others(n, me):
            recv(buf.at[j], ss.at[j], rs.at[j], at(s))
        found = merge([buf[j] for j in range(n)])
        if nxt is not None:
            nxt[nxt.shape[0] - 1] = found
    lens_total = found[0:1] + jnp.log(found[1:2])
    final_total = found[2:3] + jnp.log(found[3:4])
    apart = found[4:5] / found[3:4] + lens_total - final_total
    tall = jnp.concatenate([stack_rows([lens_total, final_total, apart]), jnp.zeros((120, 256), F32)], axis=0)
    cols[...] = tall.T
    mine = pl.ds(pl.multiple_of(half * 128 + x * 32 + quarter * 8, 8), 8)
    div[...] = jnp.broadcast_to(cols[mine, 2:3], (8, 128))

    def slopes(i, _):
        part = pl.ds(pl.multiple_of(i * 32, 32), 32)
        totals = cols[part, :]
        grad[part, :] = (
            jnp.exp(l_log[part, :] - totals[:, 0:1]) - jnp.exp(f_log[part, :] - totals[:, 1:2])
        ).astype(BF16)
        return 0

    lax.fori_loop(0, 8, slopes, 0)

    def back(yy, kk):
        block = pl.ds(pl.multiple_of((yy * 2 + kk) * COLS, 128), COLS)
        return lax.dot_general(
            grad[...], u[block, :], (((1,), (1,)), ((), ())), preferred_element_type=F32
        ).reshape(2, NX, 32, COLS)

    def away(i, _):
        c_send[i] = back(i, 1 - k)
        copy(c_send.at[i], c_recv.at[i], gc_s.at[i], gc_r.at[i], sibling).start()
        return 0

    lax.fori_loop(0, NY, away, 0)

    def home(i, _):
        acc[i] = back(i, k)
        copy(c_recv.at[i], c_recv.at[i], gc_s.at[i], gc_r.at[i], sibling).wait_recv()
        acc[i] += c_recv[i]
        return 0

    lax.fori_loop(0, NY, home, 0)
    for j, t, _ in others(NY, y):
        send(acc.at[t, 0], ry0.at[j], g1_s.at[0, j], g1_r.at[0, j], at_y(t))
    for j, t, _ in others(NX, x):
        send(acc.at[:, 1, t], rx1.at[j], g1_s.at[1, j], g1_r.at[1, j], at_x(t))
    for j, _, s in others(NY, y):
        recv(ry0.at[j], g1_s.at[0, j], g1_r.at[0, j], at_y(s))

    def add0(i, _):
        r0[i] = acc[y, 0, i] + ry0[0, i] + ry0[1, i] + ry0[2, i]
        return 0

    lax.fori_loop(0, NX, add0, 0)
    for j, t, _ in others(NX, x):
        send(r0.at[t], rx0.at[j], g2_s.at[0, j], g2_r.at[0, j], at_x(t))
    for j, _, s in others(NX, x):
        recv(rx1.at[j], g1_s.at[1, j], g1_r.at[1, j], at_x(s))

    def add1(i, _):
        r1[i] = acc[i, 1, x] + rx1[0, i] + rx1[1, i] + rx1[2, i]
        return 0

    lax.fori_loop(0, NY, add1, 0)
    for j, t, _ in others(NY, y):
        send(r1.at[t], ry1.at[j], g2_s.at[1, j], g2_r.at[1, j], at_y(t))
    for j, _, s in others(NX, x):
        recv(rx0.at[j], g2_s.at[0, j], g2_r.at[0, j], at_x(s))
    for j, _, s in others(NY, y):
        recv(ry1.at[j], g2_s.at[1, j], g2_r.at[1, j], at_y(s))
    sz[0:4] = (r0[x] + rx0[0] + rx0[1] + rx0[2]).reshape(4, 8, COLS)
    sz[4:8] = (r1[y] + ry1[0] + ry1[1] + ry1[2]).reshape(4, 8, COLS)
    for j, t, _ in others(NZ, z):
        send(sz.at[t], rz.at[j], gz_s.at[j], gz_r.at[j], at_z(t))
    state_grad = sz[z]
    for j, _, s in others(NZ, z):
        recv(rz.at[j], gz_s.at[j], gz_r.at[j], at_z(s))
        state_grad = state_grad + rz[j]

    weighted = gain_part * state_grad
    state = l_state[...]
    slope = group_sum(jnp.sum(weighted * state, axis=1, keepdims=True), w_send, w_recv, w_s, w_r) / D
    delta = inverse * weighted - state * (inverse * inverse * inverse * slope)
    sd_pack[...] = pack(delta)
    for j, t, _ in others(NZ, z):
        send(sd_pack, sd_z.at[z], oz_s.at[j], oz_r.at[j], at_z(t))
    sd_z[z] = sd_pack[...]
    for j, _, s in others(NZ, z):
        recv(sd_z.at[s], oz_s.at[j], oz_r.at[j], at_z(s))
    sd[:, x] = unpack(sd_z[...]).reshape(2, 32, COLS)
    for j, t, _ in others(NX, x):
        send(sd.at[:, x], sd.at[:, x], ox_s.at[j], ox_r.at[j], at_x(t))
    for j, _, s in others(NX, x):
        recv(sd.at[:, s], ox_s.at[j], ox_r.at[j], at_x(s))
    delta_all = sd[...].reshape(256, COLS)
    gt[...] = jnp.dot(rows_t[...], delta_all, preferred_element_type=F32)[:ROWS]
    goff[...] = jnp.sum(delta_all.astype(F32), axis=0, keepdims=True)

    for i in range(NY):
        copy(c_send.at[i], c_recv.at[i], gc_s.at[i], gc_r.at[i], sibling).wait_send()
    for one in unsent:
        one.wait_send()


def on_device(hidden, final_hidden, translator, offset, norm_gain, unembed):
    vm = pltpu.VMEM
    dma = pltpu.SemaphoreType.DMA
    blocks = [
        vm((D, VOC), BF16), vm((NZ, 16, 512), BF16), vm((NZ, 16, 512), BF16), vm((NX, 2, 32, 256), BF16),
        vm((2, NX, 32, 256), BF16), vm((256, 256), BF16), vm((256, COLS), BF16), vm((2, NX, 32, COLS), F32),
        vm((3, 2, 32, COLS), F32), vm((NZ, 8, COLS), F32), vm((7, 8, COLS), F32),
        vm((8, D), F32), vm((16, 512), BF16), vm((NZ, 16, 512), BF16), vm((2, NY, 2, NX, 32, COLS), BF16),
        vm((16, 512), BF16), vm((NZ, 16, 512), BF16), vm((2, NY, 2, NX, 32, COLS), BF16), vm((8, COLS), F32),
        vm((8, 128), F32), vm((7, 8, 128), F32), vm((8, 128), F32), vm((7, 8, 128), F32),
        vm((256, VOC), F32), vm((256, VOC), F32),
        vm((2, 8, 256), F32), vm((NY, 8, 256), F32), vm((NX, 8, 256), F32), vm((NZ, 8, 256), F32),
        vm((256, 128), F32), vm((256, VOC), BF16),
        vm((NY, 2, NX, 32, COLS), F32), vm((NY, 2, NX, 32, COLS), F32), vm((NY, 2, NX, 32, COLS), F32),
        vm((3, NX, 32, COLS), F32), vm((3, NY, 32, COLS), F32), vm((NX, 32, COLS), F32), vm((NY, 32, COLS), F32),
        vm((3, 32, COLS), F32), vm((3, 32, COLS), F32), vm((NZ, 8, COLS), F32), vm((7, 8, COLS), F32),
        vm((16, 512), BF16), vm((NZ, 16, 512), BF16), vm((2, NX, 32, COLS), BF16),
    ]
    pairs = [
        (7,), (3,), (3,), (7,), (7,), (7,),
        (7,), (2, 3), (2, 4, 3), (2, 4, 4),
        (7,), (2, 3), (2, 4, 3), (2, 4, 4),
        (), (3,), (3,), (7,),
        (4,), (2, 3), (2, 3), (7,),
        (7,), (3,),
    ]
    sems = [dma]
    for shape in pairs:
        sems += [dma(shape) if shape else dma] * 2
    whole = pl.BlockSpec(memory_space=pltpu.VMEM)
    gt, goff, div = pl.pallas_call(
        kernel,
        out_shape=(
            jax.ShapeDtypeStruct((ROWS, COLS), F32),
            jax.ShapeDtypeStruct((1, COLS), F32),
            jax.ShapeDtypeStruct((8, 128), F32),
        ),
        in_specs=[whole] * 5 + [pl.BlockSpec(memory_space=pl.ANY)],
        out_specs=(whole, whole, whole),
        scratch_shapes=blocks + sems,
        compiler_params=pltpu.CompilerParams(
            collective_id=0, has_side_effects=True, vmem_limit_bytes=56 * 2**20
        ),
        name="lens_step",
    )(hidden, final_hidden, translator, offset.reshape(1, COLS), norm_gain.reshape(1, D), unembed)
    return gt, goff.reshape(COLS), div[:, 0]


def solution(mesh):
    placed = (P("dp", None), P("dp", None), P("dp", "vocab"), P("vocab"), P(), P(None, ("dp", "vocab")))
    return jax.shard_map(
        on_device,
        mesh=mesh,
        in_specs=placed,
        out_specs=(P("dp", "vocab"), P("vocab"), P("dp")),
        check_vma=False,
    )
```

```python
import functools

import jax
import jax.numpy as jnp
from jax import lax
from jax.experimental import pallas as pl
from jax.experimental.pallas import tpu as pltpu
from jax.sharding import PartitionSpec as P

MESH = pl.DeviceIdType.MESH
F32, BF16 = jnp.float32, jnp.bfloat16
D = 7168
COLS = 896
ROWS = 224
VOC = 512
EPSILON = 1e-06
NZ, NX, NY = 8, 4, 4


def pack(a):
    low = jnp.concatenate([a[:, 512:], jnp.zeros((8, 128), F32)], axis=1)
    return jnp.concatenate([a[:, :512], low], axis=0).astype(BF16)


def unpack(blocks):
    wide = blocks.astype(F32)
    return jnp.concatenate([wide[:, :8], wide[:, 8:, :384]], axis=2).reshape(64, COLS).astype(BF16)


def merge(tiles):
    lens_peak = functools.reduce(jnp.maximum, [t[0:1] for t in tiles])
    final_peak = functools.reduce(jnp.maximum, [t[2:3] for t in tiles])
    lens_sum = sum(t[1:2] * jnp.exp(t[0:1] - lens_peak) for t in tiles)
    scales = [jnp.exp(t[2:3] - final_peak) for t in tiles]
    final_sum = sum(t[3:4] * s for t, s in zip(tiles, scales))
    cross = sum(t[4:5] * s for t, s in zip(tiles, scales))
    return stack_rows([lens_peak, lens_sum, final_peak, final_sum, cross])


def stack_rows(rows):
    place = lax.broadcasted_iota(jnp.int32, (8, 256), 0)
    tile = jnp.zeros((8, 256), F32)
    for i, row in enumerate(rows):
        tile = jnp.where(place == i, jnp.broadcast_to(row, (8, 256)), tile)
    return tile


def kernel(
    hid, fin, tw, off, gain, unemb, rows_out, sd_out, div,
    u, hpack, hin, twp, mapped, mapped_b, cx, sx, dz,
    f_norm, f_pack, f_z, f_buf, l_pack, l_z, l_buf, l_state, regain, squares,
    l_log, f_log, st_core, st_x, st_z, sl_core, sl_y, sl_x, sl_z, cols, inv_cols, sl_cols, grad,
    c_send, c_recv, acc, ry0, rx1, r0, r1, rx0, ry1, sz, rz,
    sd_z,
    u_sem, a_s, a_r, c_s, c_r, d_s, d_r,
    fz_s, fz_r, f1_s, f1_r, f2_s, f2_r, fc_s, fc_r,
    lz_s, lz_r, l1_s, l1_r, l2_s, l2_r, lc_s, lc_r,
    tc_s, tc_r, tx_s, tx_r, tz_s, tz_r,
    pc_s, pc_r, py_s, py_r, px_s, px_r, pz_s, pz_r,
    gc_s, gc_r, gy_s, gy_r, gx_s, gx_r, g2_s, g2_r, gz_s, gz_r,
    oz_s, oz_r, ox_s, ox_r,
):
    r, c = lax.axis_index("dp"), lax.axis_index("vocab")
    z, x = lax.div(r, NX), lax.rem(r, NX)
    y, k = lax.div(c, 2), lax.rem(c, 2)
    half, quarter = lax.div(z, 4), lax.rem(z, 4)
    feat = pl.ds(pl.multiple_of(c * COLS, 128), COLS)

    def at_z(i):
        return (i * NX + x, c)

    def at_x(i):
        return (z * NX + i, c)

    def at_y(i):
        return (r, i * 2 + k)

    sibling = (r, y * 2 + (1 - k))
    unsent = []

    def copy(src, dst, ss, rs, dev):
        return pltpu.make_async_remote_copy(
            src_ref=src, dst_ref=dst, send_sem=ss, recv_sem=rs, device_id=dev, device_id_type=MESH
        )

    def pair(sem):
        ss, rs, at = sem
        return (ss.at[at], rs.at[at]) if at else (ss, rs)

    def send(src, dst, sem, dev):
        one = copy(src, dst, *pair(sem), dev)
        one.start()
        unsent.append(one)

    def recv(land, sem, dev):
        copy(land, land, *pair(sem), dev).wait_recv()

    def others(n, me):
        return [(d - 1, lax.rem(me + d, n), lax.rem(me + (n - d), n)) for d in range(1, n)]

    barrier = pltpu.get_barrier_semaphore()
    def slot_of(i, j):
        return lax.div(i, 4) * 16 + j * 4 + lax.rem(i, 4)

    plane = []
    for i in range(NZ):
        for j in range(NX):
            if i + j:
                ahead = (lax.rem(z + i, NZ), lax.rem(x + j, NX))
                behind = (lax.rem(z + (NZ - i), NZ), lax.rem(x + (NX - j), NX))
                plane.append((len(plane), ahead, behind))
    partners = [(zz * NX + xx, c) for _, (zz, xx), _ in plane]
    group = [(d - 1, (r, lax.rem(c + d, 8)), (r, lax.rem(c + (8 - d), 8))) for d in range(1, 8)]
    partners += [t for _, t, _ in group]
    for p in partners:
        pl.semaphore_signal(barrier, inc=1, device_id=p, device_id_type=MESH)
    load_u = pltpu.make_async_copy(unemb, u, u_sem)
    load_u.start()

    flat = hid[...].astype(F32)
    for i in range(NZ * NX):
        low = jnp.concatenate([flat[:, i * ROWS + 128 : (i + 1) * ROWS], jnp.zeros((8, 32), F32)], axis=1)
        hpack[i] = jnp.concatenate([flat[:, i * ROWS : i * ROWS + 128], low], axis=0).astype(BF16)
    wide = fin[...].astype(F32)
    final_inverse = lax.rsqrt(jnp.sum(wide * wide, axis=1, keepdims=True) / D + EPSILON)
    gain_all = gain[...].astype(F32).reshape(1, D)
    f_norm[...] = wide * final_inverse * gain_all
    f_pack[...] = pack(f_norm[:, feat])
    for i in range(8):
        regain[i] = jnp.broadcast_to(1.0 / gain_all[:, i * COLS : (i + 1) * COLS], (8, COLS))
    twp[:ROWS] = tw[...]
    twp[ROWS:] = jnp.zeros((256 - ROWS, COLS), BF16)
    pl.semaphore_wait(barrier, len(partners))

    mine8 = slot_of(z, x)
    for j, (zz, xx), _ in plane:
        send(hpack.at[zz * NX + xx], hin.at[mine8], (a_s, a_r, (j,)), (zz * NX + xx, c))
    for j, t, _ in others(NZ, z):
        send(f_pack, f_z.at[z], (fz_s, fz_r, (j,)), at_z(t))
    hin[mine8] = hpack[r]
    f_z[z] = f_pack[...]

    f_first, l_first = ("x", "x"), ("x", "y")

    def own_pieces(buf, zbuf, zs, zr, s1, r1, s2, r2, sc, rc, firsts):
        for j, _, s in others(NZ, z):
            recv(zbuf.at[s], (zs, zr, (j,)), at_z(s))
        flat = unpack(zbuf[...])
        for h in range(2):
            buf[k, y, h, x] = flat[h * 32 : (h + 1) * 32]
        for h, first in enumerate(firsts):
            piece = buf.at[k, y, h, x]
            ways = [(NX, x, at_x), (NY, y, at_y)]
            (n1, m1, at1), (n2, m2, at2) = ways if first == "x" else ways[::-1]
            for j, t, _ in others(n1, m1):
                send(piece, piece, (s1, r1, (h, j)), at1(t))
            for j, t, _ in others(n2, m2):
                send(piece, piece, (s2, r2, (h, 0, j)), at2(t))
            send(piece, piece, (sc, rc, (h, 0, 0)), sibling)

    def forward(buf, s1, r1, s2, r2, sc, rc, firsts):
        for q in range(1, 4):
            for h, first in enumerate(firsts):
                if first == "x":
                    s = lax.rem(x + (NX - q), NX)
                    piece, dev, n2, m2, at2 = buf.at[k, y, h, s], at_x(s), NY, y, at_y
                    slot = (h, 0, q)
                else:
                    s = lax.rem(y + (NY - q), NY)
                    piece, dev, n2, m2, at2 = buf.at[k, s, h, x], at_y(s), NX, x, at_x
                    slot = (h, q, 0)
                recv(piece, (s1, r1, (h, q - 1)), dev)
                for j, t, _ in others(n2, m2):
                    send(piece, piece, (s2, r2, (h, q, j)), at2(t))
                send(piece, piece, (sc, rc, slot), sibling)

    def rest(buf, s2, r2, sc, rc, firsts, each=lambda q: None):
        for q in range(1, 4):
            for j in range(4):
                for h, first in enumerate(firsts):
                    if first == "x":
                        yy, xx = lax.rem(y + (NY - q), NY), lax.rem(x + (NX - j), NX)
                        dev, slot = at_y(yy), (h, q, j)
                    else:
                        yy, xx = lax.rem(y + (NY - j), NY), lax.rem(x + (NX - q), NX)
                        dev, slot = at_x(xx), (h, j, q)
                    piece = buf.at[k, yy, h, xx]
                    recv(piece, (s2, r2, (h, j, q - 1)), dev)
                    send(piece, piece, (sc, rc, slot), sibling)
            each(q)

    def logits(buf, log, kk, yy):
        cc = yy * 2 + kk
        block = pl.ds(pl.multiple_of(cc * COLS, 128), COLS)
        value = buf[kk, yy].reshape(256, COLS)
        log[...] += jnp.dot(value, u[block, :], preferred_element_type=F32)
        if buf is l_buf:
            scale = regain[cc][0:1]
            total = squares[...]
            for i in range(COLS // 128):
                lanes = slice(i * 128, (i + 1) * 128)
                plain = value[:, lanes].astype(F32) * scale[:, lanes]
                total = total + plain * plain
            squares[...] = total

    def own_logits(buf, log):
        def step(q, _):
            logits(buf, log, k, lax.rem(y + (NY - q), NY))
            return 0

        lax.fori_loop(0, NY, step, 0)

    def sibling_logits(buf, log, sc, rc):
        def step(q, _):
            yy = lax.rem(y + (NY - q), NY)
            for h in range(2):
                for j in range(4):
                    xx = lax.rem(x + (NX - j), NX)
                    recv(buf.at[1 - k, yy, h, xx], (sc, rc, (h, q, j)), sibling)
            logits(buf, log, 1 - k, yy)
            return 0

        lax.fori_loop(0, NY, step, 0)

    for j, _, (zz, xx) in plane:
        recv(hin.at[slot_of(zz, xx)], (a_s, a_r, (j,)), (zz * NX + xx, c))
    found = hin[...].astype(F32)
    rows = jnp.concatenate([found[:, :8].reshape(256, 128), found[:, 8:].reshape(256, 128)], axis=1)
    product = jnp.dot(rows.astype(BF16), twp[...], preferred_element_type=F32)
    mapped[...] = product.reshape(2, NX, 32, COLS)
    mapped_b[...] = product.astype(BF16).reshape(2, NX, 32, COLS)
    for j, t, _ in others(NX, x):
        send(mapped_b.at[:, t], cx.at[j], (c_s, c_r, (j,)), at_x(t))
    own_pieces(f_buf, f_z, fz_s, fz_r, f1_s, f1_r, f2_s, f2_r, fc_s, fc_r, f_first)
    rows_out[...] = rows.T.astype(BF16)
    squares[...] = jnp.zeros_like(squares)
    l_log[...] = jnp.zeros_like(l_log)
    f_log[...] = jnp.zeros_like(f_log)
    for j, t, s in others(NX, x):
        recv(cx.at[j], (c_s, c_r, (j,)), at_x(s))
    sx[...] = (mapped[:, x] + cx[0].astype(F32) + cx[1].astype(F32) + cx[2].astype(F32)).reshape(NZ, 8, COLS)
    for j, t, _ in others(NZ, z):
        send(sx.at[t], dz.at[j], (d_s, d_r, (j,)), at_z(t))
    forward(f_buf, f1_s, f1_r, f2_s, f2_r, fc_s, fc_r, f_first)
    base = hid[:, feat].astype(F32) + off[...].reshape(1, COLS) + sx[z]
    gain_part = 1.0 / regain[c]
    for j, _, s in others(NZ, z):
        recv(dz.at[j], (d_s, d_r, (j,)), at_z(s))
        base = base + dz[j]
    l_state[...] = base

    l_pack[...] = pack(base * gain_part)
    for j, t, _ in others(NZ, z):
        send(l_pack, l_z.at[z], (lz_s, lz_r, (j,)), at_z(t))
    l_z[z] = l_pack[...]
    load_u.wait()
    rest(f_buf, f2_s, f2_r, fc_s, fc_r, f_first)
    own_pieces(l_buf, l_z, lz_s, lz_r, l1_s, l1_r, l2_s, l2_r, lc_s, lc_r, l_first)
    own_logits(f_buf, f_log)
    forward(l_buf, l1_s, l1_r, l2_s, l2_r, lc_s, lc_r, l_first)
    sibling_logits(f_buf, f_log, fc_s, fc_r)
    rest(l_buf, l2_s, l2_r, lc_s, lc_r, l_first)
    own_logits(l_buf, l_log)
    sibling_logits(l_buf, l_log, lc_s, lc_r)

    place = lax.broadcasted_iota(jnp.int32, (32, 128), 1)

    def local(i, _):
        part = pl.ds(pl.multiple_of(i * 32, 32), 32)
        mean = jnp.sum(squares[part, :], axis=1, keepdims=True) / D
        inverse = lax.rsqrt(mean + EPSILON)
        inv_cols[part, :] = jnp.broadcast_to(inverse, (32, 128))
        a, b = l_log[part, :] * inverse, f_log[part, :]
        l_log[part, :] = a
        a_peak, b_peak = jnp.max(a, axis=1, keepdims=True), jnp.max(b, axis=1, keepdims=True)
        weight = jnp.exp(b - b_peak)
        found = [
            a_peak, jnp.sum(jnp.exp(a - a_peak), axis=1, keepdims=True), b_peak,
            jnp.sum(weight, axis=1, keepdims=True), jnp.sum(weight * (b - a), axis=1, keepdims=True),
        ]
        tile = jnp.zeros((32, 128), F32)
        for n, v in enumerate(found):
            tile = jnp.where(place == n, jnp.broadcast_to(v, (32, 128)), tile)
        cols[part, :] = tile
        return 0

    lax.fori_loop(0, 8, local, 0)
    st_core[7] = cols[...].T[:8]
    for j, t, _ in group:
        send(st_core.at[7], st_core.at[j], (tc_s, tc_r, (j,)), t)
    for j, _, s in group:
        recv(st_core.at[j], (tc_s, tc_r, (j,)), s)
    found = merge([st_core[j] for j in range(8)])
    for buf, n, me, at, ss, rs in ((st_x, NX, x, at_x, tx_s, tx_r), (st_z, NZ, z, at_z, tz_s, tz_r)):
        buf[n - 1] = found
        for j, t, _ in others(n, me):
            send(buf.at[n - 1], buf.at[j], (ss, rs, (j,)), at(t))
        for j, _, s in others(n, me):
            recv(buf.at[j], (ss, rs, (j,)), at(s))
        found = merge([buf[j] for j in range(n)])
    lens_total = found[0:1] + jnp.log(found[1:2])
    final_total = found[2:3] + jnp.log(found[3:4])
    apart = found[4:5] / found[3:4] + lens_total - final_total
    tall = jnp.concatenate([stack_rows([lens_total, final_total, apart]), jnp.zeros((120, 256), F32)], axis=0)
    cols[...] = tall.T
    mine = pl.ds(pl.multiple_of(half * 128 + x * 32 + quarter * 8, 8), 8)
    div[...] = jnp.broadcast_to(cols[mine, 2:3], (8, 128))

    def slopes(i, _):
        part = pl.ds(pl.multiple_of(i * 32, 32), 32)
        totals = cols[part, :]
        a = l_log[part, :]
        rounded = (jnp.exp(a - totals[:, 0:1]) - jnp.exp(f_log[part, :] - totals[:, 1:2])).astype(BF16)
        grad[part, :] = rounded
        slope = jnp.sum(rounded.astype(F32) * a, axis=1, keepdims=True)
        sl_cols[part, :] = jnp.broadcast_to(slope, (32, 128))
        return 0

    lax.fori_loop(0, 8, slopes, 0)

    def back(yy, kk):
        block = pl.ds(pl.multiple_of((yy * 2 + kk) * COLS, 128), COLS)
        return lax.dot_general(
            grad[...], u[block, :], (((1,), (1,)), ((), ())), preferred_element_type=F32
        ).reshape(2, NX, 32, COLS)

    def slope_send(buf, n, me, at, ss, rs):
        for j, t, _ in others(n, me):
            send(buf.at[n - 1], buf.at[j], (ss, rs, (j,)), at(t))

    def slope_sum(buf, n, me, at, ss, rs):
        total = buf[n - 1]
        for j, _, s in others(n, me):
            recv(buf.at[j], (ss, rs, (j,)), at(s))
            total = total + buf[j]
        return total

    over_y = (sl_y, NY, y, at_y, py_s, py_r)
    over_x = (sl_x, NX, x, at_x, px_s, px_r)
    over_z = (sl_z, NZ, z, at_z, pz_s, pz_r)
    sl_core[0] = sl_cols[...].T[:8]
    send(sl_core.at[0], sl_core.at[1], (pc_s, pc_r, ()), sibling)

    def block_y(i):
        return lax.rem(y + 1 + i, NY)

    def hand_over(i):
        return copy(c_send.at[i], c_recv.at[i], gc_s.at[i], gc_r.at[i], sibling)

    def y_first(i):
        return copy(acc.at[i, 0], ry0.at[i], gy_s.at[i], gy_r.at[i], at_y(block_y(i)))

    def x_first(i, j, t):
        return copy(acc.at[i, 1, t], rx1.at[j, i], gx_s.at[j, i], gx_r.at[j, i], at_x(t))

    def away(i):
        c_send[i] = back(block_y(i), 1 - k)
        hand_over(i).start()

    away(0)

    def home(i, _):
        @pl.when(i < NY - 1)
        def _():
            away(i + 1)

        acc[i] = back(block_y(i), k)
        hand_over(i).wait_recv()
        acc[i] += c_recv[i]

        @pl.when(i < NY - 1)
        def _():
            y_first(i).start()

        for j, t, _ in others(NX, x):
            x_first(i, j, t).start()
        return 0

    lax.fori_loop(0, NY, home, 0)
    recv(sl_core.at[1], (pc_s, pc_r, ()), sibling)
    sl_y[NY - 1] = sl_core[0] + sl_core[1]
    slope_send(*over_y)
    for i in range(NY - 1):
        y_first(i).wait_recv()

    def add0(i, _):
        r0[i] = acc[NY - 1, 0, i] + ry0[0, i] + ry0[1, i] + ry0[2, i]
        return 0

    lax.fori_loop(0, NX, add0, 0)
    for j, t, _ in others(NX, x):
        send(r0.at[t], rx0.at[j], (g2_s, g2_r, (0, j)), at_x(t))
    sl_x[NX - 1] = slope_sum(*over_y)
    slope_send(*over_x)

    for i in range(NY):
        for j, t, _ in others(NX, x):
            x_first(i, j, t).wait_recv()
        r1[i] = acc[i, 1, x] + rx1[0, i] + rx1[1, i] + rx1[2, i]
        if i < NY - 1:
            send(r1.at[i], ry1.at[i], (g2_s, g2_r, (1, i)), at_y(block_y(i)))
    for j, _, s in others(NX, x):
        recv(rx0.at[j], (g2_s, g2_r, (0, j)), at_x(s))
    for i in range(NY - 1):
        recv(ry1.at[i], (g2_s, g2_r, (1, i)), at_y(block_y(i)))
    sz[0:4] = (r0[x] + rx0[0] + rx0[1] + rx0[2]).reshape(4, 8, COLS)
    sz[4:8] = (r1[NY - 1] + ry1[0] + ry1[1] + ry1[2]).reshape(4, 8, COLS)
    for j, t, _ in others(NZ, z):
        send(sz.at[t], rz.at[j], (gz_s, gz_r, (j,)), at_z(t))
    sl_z[NZ - 1] = slope_sum(*over_x)
    slope_send(*over_z)
    state_grad = sz[z]
    for j, _, s in others(NZ, z):
        recv(rz.at[j], (gz_s, gz_r, (j,)), at_z(s))
        state_grad = state_grad + rz[j]
    cols[...] = jnp.concatenate([slope_sum(*over_z), jnp.zeros((120, 256), F32)], axis=0).T
    inverse = inv_cols[mine, 0:1]
    slope = cols[mine, 0:1] / D
    delta = inverse * (gain_part * state_grad) - l_state[...] * (inverse * inverse * slope)
    sd_z[mine8] = pack(delta)
    own = sd_z.at[mine8]
    for j, t, _ in others(NZ, z):
        send(own, own, (oz_s, oz_r, (j,)), at_z(t))
    for j, t, _ in others(NX, x):
        send(own, own, (ox_s, ox_r, (0, j)), at_x(t))
    for q, _, s in others(NZ, z):
        piece = sd_z.at[slot_of(s, x)]
        recv(piece, (oz_s, oz_r, (q,)), at_z(s))
        for j, t, _ in others(NX, x):
            send(piece, piece, (ox_s, ox_r, (q + 1, j)), at_x(t))
    for q in range(NZ):
        for j, _, s in others(NX, x):
            piece = sd_z.at[slot_of(lax.rem(z + (NZ - q), NZ), s)]
            recv(piece, (ox_s, ox_r, (q, j)), at_x(s))
    found = sd_z[...].astype(F32)
    sd_out[...] = jnp.concatenate([found[:, :8], found[:, 8:, :384]], axis=2).reshape(256, COLS).astype(BF16)

    for i in range(NY):
        hand_over(i).wait_send()
        if i < NY - 1:
            y_first(i).wait_send()
        for j, t, _ in others(NX, x):
            x_first(i, j, t).wait_send()
    for one in unsent:
        one.wait_send()


def finish(rows, delta, div, gt, goff, divergence):
    gt[...] = jnp.dot(rows[...], delta[...], preferred_element_type=F32)[:ROWS]
    goff[...] = jnp.sum(delta[...].astype(F32), axis=0)
    divergence[...] = div[...].T[0]


def on_device(hidden, final_hidden, translator, offset, norm_gain, unembed):
    vm = pltpu.VMEM
    dma = pltpu.SemaphoreType.DMA
    blocks = [
        vm((D, VOC), BF16), vm((32, 16, 128), BF16), vm((32, 16, 128), BF16), vm((256, COLS), BF16),
        vm((2, NX, 32, COLS), F32), vm((2, NX, 32, COLS), BF16), vm((3, 2, 32, COLS), BF16),
        vm((NZ, 8, COLS), F32), vm((7, 8, COLS), F32),
        vm((8, D), F32), vm((16, 512), BF16), vm((NZ, 16, 512), BF16), vm((2, NY, 2, NX, 32, COLS), BF16),
        vm((16, 512), BF16), vm((NZ, 16, 512), BF16), vm((2, NY, 2, NX, 32, COLS), BF16), vm((8, COLS), F32),
        vm((8, 8, COLS), F32), vm((256, 128), F32),
        vm((256, VOC), F32), vm((256, VOC), F32),
        vm((8, 8, 256), F32), vm((NX, 8, 256), F32), vm((NZ, 8, 256), F32),
        vm((2, 8, 256), F32), vm((NY, 8, 256), F32), vm((NX, 8, 256), F32), vm((NZ, 8, 256), F32),
        vm((256, 128), F32), vm((256, 128), F32), vm((256, 128), F32), vm((256, VOC), BF16),
        vm((NY, 2, NX, 32, COLS), F32), vm((NY, 2, NX, 32, COLS), F32), vm((NY, 2, NX, 32, COLS), F32),
        vm((3, NX, 32, COLS), F32), vm((3, NY, 32, COLS), F32), vm((NX, 32, COLS), F32), vm((NY, 32, COLS), F32),
        vm((3, 32, COLS), F32), vm((3, 32, COLS), F32), vm((NZ, 8, COLS), F32), vm((7, 8, COLS), F32),
        vm((32, 16, 512), BF16),
    ]
    pairs = [
        (31,), (3,), (7,),
        (7,), (2, 3), (2, 4, 3), (2, 4, 4),
        (7,), (2, 3), (2, 4, 3), (2, 4, 4),
        (7,), (3,), (7,),
        (), (3,), (3,), (7,),
        (4,), (3,), (3, 4), (2, 3), (7,),
        (7,), (8, 3),
    ]
    sems = [dma]
    for shape in pairs:
        sems += [dma(shape) if shape else dma] * 2
    whole = pl.BlockSpec(memory_space=pltpu.VMEM)
    rows, delta, div = pl.pallas_call(
        kernel,
        out_shape=(
            jax.ShapeDtypeStruct((256, 256), BF16),
            jax.ShapeDtypeStruct((256, COLS), BF16),
            jax.ShapeDtypeStruct((8, 128), F32),
        ),
        in_specs=[whole] * 5 + [pl.BlockSpec(memory_space=pl.ANY)],
        out_specs=(whole, whole, whole),
        scratch_shapes=blocks + sems,
        compiler_params=pltpu.CompilerParams(
            collective_id=0, has_side_effects=True, vmem_limit_bytes=56 * 2**20
        ),
        name="lens_step",
    )(hidden, final_hidden, translator, offset, norm_gain, unembed)
    return pl.pallas_call(
        finish,
        out_shape=(
            jax.ShapeDtypeStruct((ROWS, COLS), F32),
            jax.ShapeDtypeStruct((COLS,), F32),
            jax.ShapeDtypeStruct((8,), F32),
        ),
        in_specs=[whole] * 3,
        out_specs=(whole, whole, whole),
        name="finish",
    )(rows, delta, div)


def solution(mesh):
    placed = (P("dp", None), P("dp", None), P("dp", "vocab"), P("vocab"), P(), P(None, ("dp", "vocab")))
    return jax.shard_map(
        on_device,
        mesh=mesh,
        in_specs=placed,
        out_specs=(P("dp", "vocab"), P("vocab"), P("dp")),
        check_vma=False,
    )
```

```python
import functools

import jax
import jax.numpy as jnp
from jax import lax
from jax.experimental import pallas as pl
from jax.experimental.pallas import tpu as pltpu
from jax.sharding import PartitionSpec as P

MESH = pl.DeviceIdType.MESH
F32, BF16 = jnp.float32, jnp.bfloat16
D = 7168
COLS = 896
ROWS = 224
VOC = 512
EPSILON = 1e-06
NZ, NX, NY = 8, 4, 4


def pack(a):
    low = jnp.concatenate([a[:, 512:], jnp.zeros((8, 128), F32)], axis=1)
    return jnp.concatenate([a[:, :512], low], axis=0).astype(BF16)


def unpack(blocks):
    wide = blocks.astype(F32)
    return jnp.concatenate([wide[:, :8], wide[:, 8:, :384]], axis=2).reshape(64, COLS).astype(BF16)


def merge(tiles):
    lens_peak = functools.reduce(jnp.maximum, [t[0:1] for t in tiles])
    final_peak = functools.reduce(jnp.maximum, [t[2:3] for t in tiles])
    lens_sum = sum(t[1:2] * jnp.exp(t[0:1] - lens_peak) for t in tiles)
    scales = [jnp.exp(t[2:3] - final_peak) for t in tiles]
    final_sum = sum(t[3:4] * s for t, s in zip(tiles, scales))
    cross = sum(t[4:5] * s for t, s in zip(tiles, scales))
    return stack_rows([lens_peak, lens_sum, final_peak, final_sum, cross])


def stack_rows(rows):
    place = lax.broadcasted_iota(jnp.int32, (8, 256), 0)
    tile = jnp.zeros((8, 256), F32)
    for i, row in enumerate(rows):
        tile = jnp.where(place == i, jnp.broadcast_to(row, (8, 256)), tile)
    return tile


def kernel(
    hid_in, fin_in, tw_in, off_in, gain_in, unemb, rows_out, sd_out, div,
    hid, fin, off, gain, u, hpack, hin, twp, mapped, mapped_b, cx, sx, dz,
    f_norm, f_pack, f_z, f_buf, l_pack, l_z, l_buf, l_state, gains, regain, squares,
    l_log, f_log, st_core, st_x, st_z, sl_core, sl_y, sl_x, sl_z, cols, inv_cols, sl_cols, grad,
    c_send, c_recv, acc, fy, ry, fx, rx, r0, r1, rx0, ry1, sz, rz,
    sd_z,
    in_sem, a_s, a_r, c_s, c_r, d_s, d_r,
    fz_s, fz_r, f1_s, f1_r, f2_s, f2_r, fc_s, fc_r,
    lz_s, lz_r, l1_s, l1_r, l2_s, l2_r, lc_s, lc_r,
    tc_s, tc_r, tx_s, tx_r, tz_s, tz_r,
    pc_s, pc_r, py_s, py_r, px_s, px_r, pz_s, pz_r,
    gc_s, gc_r, yf_s, yf_r, yn_s, yn_r, xf_s, xf_r, xn_s, xn_r, xs_s, xs_r, g2_s, g2_r, gz_s, gz_r,
    oz_s, oz_r, ox_s, ox_r,
):
    r, c = lax.axis_index("dp"), lax.axis_index("vocab")
    z, x = lax.div(r, NX), lax.rem(r, NX)
    y, k = lax.div(c, 2), lax.rem(c, 2)
    half, quarter = lax.div(z, 4), lax.rem(z, 4)
    feat = pl.ds(pl.multiple_of(c * COLS, 128), COLS)

    def at_z(i):
        return (i * NX + x, c)

    def at_x(i):
        return (z * NX + i, c)

    def at_y(i):
        return (r, i * 2 + k)

    sibling = (r, y * 2 + (1 - k))
    unsent = []

    def copy(src, dst, ss, rs, dev):
        return pltpu.make_async_remote_copy(
            src_ref=src, dst_ref=dst, send_sem=ss, recv_sem=rs, device_id=dev, device_id_type=MESH
        )

    def pair(sem):
        ss, rs, at = sem
        return (ss.at[at], rs.at[at]) if at else (ss, rs)

    def send(src, dst, sem, dev):
        one = copy(src, dst, *pair(sem), dev)
        one.start()
        unsent.append(one)

    def recv(land, sem, dev):
        copy(land, land, *pair(sem), dev).wait_recv()

    def others(n, me):
        return [(d - 1, lax.rem(me + d, n), lax.rem(me + (n - d), n)) for d in range(1, n)]

    barrier = pltpu.get_barrier_semaphore()
    def slot_of(i, j):
        return lax.div(i, 4) * 16 + j * 4 + lax.rem(i, 4)

    plane = []
    for i in range(NZ):
        for j in range(NX):
            if i + j:
                ahead = (lax.rem(z + i, NZ), lax.rem(x + j, NX))
                behind = (lax.rem(z + (NZ - i), NZ), lax.rem(x + (NX - j), NX))
                plane.append((len(plane), ahead, behind))
    partners = [(zz * NX + xx, c) for _, (zz, xx), _ in plane]
    group = [(d - 1, (r, lax.rem(c + d, 8)), (r, lax.rem(c + (8 - d), 8))) for d in range(1, 8)]
    partners += [t for _, t, _ in group]
    for p in partners:
        pl.semaphore_signal(barrier, inc=1, device_id=p, device_id_type=MESH)
    pairs = [(hid_in, hid), (fin_in, fin), (gain_in, gain), (tw_in, twp.at[pl.ds(0, ROWS)]), (off_in, off), (unemb, u)]
    loads = [pltpu.make_async_copy(src, dst, in_sem.at[i]) for i, (src, dst) in enumerate(pairs)]
    load_hid, load_fin, load_gain, load_tw, load_off, load_u = loads
    for load in loads:
        load.start()
    load_hid.wait()

    flat = hid[...].astype(F32)
    for i in range(NZ * NX):
        low = jnp.concatenate([flat[:, i * ROWS + 128 : (i + 1) * ROWS], jnp.zeros((8, 32), F32)], axis=1)
        hpack[i] = jnp.concatenate([flat[:, i * ROWS : i * ROWS + 128], low], axis=0).astype(BF16)
    pl.semaphore_wait(barrier, len(partners))

    mine8 = slot_of(z, x)
    for j, (zz, xx), _ in plane:
        send(hpack.at[zz * NX + xx], hin.at[mine8], (a_s, a_r, (j,)), (zz * NX + xx, c))
    hin[mine8] = hpack[r]
    load_fin.wait()
    load_gain.wait()
    wide = fin[...].astype(F32)
    final_inverse = lax.rsqrt(jnp.sum(wide * wide, axis=1, keepdims=True) / D + EPSILON)
    gain_all = gain[...].astype(F32).reshape(1, D)
    f_norm[...] = wide * final_inverse * gain_all
    f_pack[...] = pack(f_norm[:, feat])
    for i in range(8):
        gains[i] = jnp.broadcast_to(gain_all[:, i * COLS : (i + 1) * COLS], (8, COLS))
        regain[i] = 1.0 / gains[i]
    twp[ROWS:] = jnp.zeros((256 - ROWS, COLS), BF16)
    for j, t, _ in others(NZ, z):
        send(f_pack, f_z.at[z], (fz_s, fz_r, (j,)), at_z(t))
    f_z[z] = f_pack[...]

    f_first, l_first = ("x", "y"), ("x", "y")

    def own_pieces(buf, flat, s1, r1, s2, r2, sc, rc, firsts):
        for h in range(2):
            buf[k, y, h, x] = flat[h * 32 : (h + 1) * 32]
        for stage in range(2):
            for h, first in enumerate(firsts):
                piece = buf.at[k, y, h, x]
                along_x = (first == "x") == (stage == 0)
                n, me, at = (NX, x, at_x) if along_x else (NY, y, at_y)
                for j, t, _ in others(n, me):
                    sem = (s1, r1, (h, j)) if stage == 0 else (s2, r2, (h, 0, j))
                    send(piece, piece, sem, at(t))
        for h in range(2):
            piece = buf.at[k, y, h, x]
            send(piece, piece, (sc, rc, (h, 0, 0)), sibling)

    def forward(buf, s1, r1, s2, r2, sc, rc, firsts):
        for q in (1, 3, 2):
            for h, first in enumerate(firsts):
                if first == "x":
                    s = lax.rem(x + (NX - q), NX)
                    piece, dev, n2, m2, at2 = buf.at[k, y, h, s], at_x(s), NY, y, at_y
                    slot = (h, 0, q)
                else:
                    s = lax.rem(y + (NY - q), NY)
                    piece, dev, n2, m2, at2 = buf.at[k, s, h, x], at_y(s), NX, x, at_x
                    slot = (h, q, 0)
                recv(piece, (s1, r1, (h, q - 1)), dev)
                for j, t, _ in others(n2, m2):
                    send(piece, piece, (s2, r2, (h, q, j)), at2(t))
                send(piece, piece, (sc, rc, slot), sibling)

    def rest(buf, s2, r2, sc, rc, firsts):
        for j in (0, 1, 3, 2):
            for q in (1, 3, 2):
                for h, first in enumerate(firsts):
                    if first == "x":
                        yy, xx = lax.rem(y + (NY - q), NY), lax.rem(x + (NX - j), NX)
                        dev, slot = at_y(yy), (h, q, j)
                    else:
                        yy, xx = lax.rem(y + (NY - j), NY), lax.rem(x + (NX - q), NX)
                        dev, slot = at_x(xx), (h, j, q)
                    piece = buf.at[k, yy, h, xx]
                    recv(piece, (s2, r2, (h, j, q - 1)), dev)
                    send(piece, piece, (sc, rc, slot), sibling)

    def all_logits(buf, log, sc, rc):
        def step(n, _):
            q = lax.rem(n, NY)
            yy, kk = lax.rem(y + (NY - q), NY), jnp.where(n < NY, k, 1 - k)

            @pl.when(n >= NY)
            def _():
                for h in range(2):
                    for j in range(4):
                        xx = lax.rem(x + (NX - j), NX)
                        recv(buf.at[1 - k, yy, h, xx], (sc, rc, (h, q, j)), sibling)

            cc = yy * 2 + kk
            block = pl.ds(pl.multiple_of(cc * COLS, 128), COLS)
            value = buf[kk, yy].reshape(256, COLS)
            log[...] += jnp.dot(value, u[block, :], preferred_element_type=F32)
            if buf is l_buf:
                scale = regain[cc][0:1]
                total = squares[...]
                for i in range(COLS // 128):
                    lanes = slice(i * 128, (i + 1) * 128)
                    plain = value[:, lanes].astype(F32) * scale[:, lanes]
                    total = total + plain * plain
                squares[...] = total
            return 0

        lax.fori_loop(0, 8, step, 0)

    for j, _, (zz, xx) in plane:
        recv(hin.at[slot_of(zz, xx)], (a_s, a_r, (j,)), (zz * NX + xx, c))
    found = hin[...].astype(F32)
    load_tw.wait()
    rows = jnp.concatenate([found[:, :8].reshape(256, 128), found[:, 8:].reshape(256, 128)], axis=1)
    product = jnp.dot(rows.astype(BF16), twp[...], preferred_element_type=F32)
    mapped[...] = product.reshape(2, NX, 32, COLS)
    mapped_b[...] = product.astype(BF16).reshape(2, NX, 32, COLS)
    quarters = [(h, pl.ds(16 * p, 16)) for h in range(2) for p in range(2)]
    for p, (h, part) in enumerate(quarters):
        for j, t, _ in others(NX, x):
            send(mapped_b.at[h, t, part], cx.at[j, h, part], (c_s, c_r, (p, j)), at_x(t))

    def z_sum(src, dst, ss, rs, zz):
        place = lax.rem(zz - z + NZ, NZ) - 1
        return copy(src.at[zz], dst.at[place], ss.at[place], rs.at[place], at_z(zz))

    def z_send(src, dst, ss, rs, zz):
        @pl.when(z != zz)
        def _():
            z_sum(src, dst, ss, rs, zz).start()

    for j, _, s in others(NZ, z):
        recv(f_z.at[s], (fz_s, fz_r, (j,)), at_z(s))
    own_pieces(f_buf, unpack(f_z[...]), f1_s, f1_r, f2_s, f2_r, fc_s, fc_r, f_first)
    rows_out[...] = rows.T.astype(BF16)
    for p, (h, part) in enumerate(quarters):
        for j, _, s in others(NX, x):
            recv(cx.at[j, h, part], (c_s, c_r, (p, j)), at_x(s))
        total = mapped[h, x, part]
        for j in range(3):
            total = total + cx[j, h, part].astype(F32)
        sx[2 * p : 2 * p + 2] = total.reshape(2, 8, COLS)
        z_send(sx, dz, d_s, d_r, 2 * p)
        z_send(sx, dz, d_s, d_r, 2 * p + 1)
    load_off.wait()
    forward(f_buf, f1_s, f1_r, f2_s, f2_r, fc_s, fc_r, f_first)
    base = hid[:, feat].astype(F32) + off[...].reshape(1, COLS) + sx[z]
    gain_part = gains[c]
    for j, _, s in others(NZ, z):
        recv(dz.at[j], (d_s, d_r, (j,)), at_z(s))
        base = base + dz[j]
    l_state[...] = base

    l_pack[...] = pack(base * gain_part)
    for j, t, _ in others(NZ, z):
        send(l_pack, l_z.at[z], (lz_s, lz_r, (j,)), at_z(t))
    l_z[z] = l_pack[...]
    squares[...] = jnp.zeros_like(squares)
    l_log[...] = jnp.zeros_like(l_log)
    f_log[...] = jnp.zeros_like(f_log)
    for j, _, s in others(NZ, z):
        recv(l_z.at[s], (lz_s, lz_r, (j,)), at_z(s))
    own_pieces(l_buf, unpack(l_z[...]), l1_s, l1_r, l2_s, l2_r, lc_s, lc_r, l_first)
    forward(l_buf, l1_s, l1_r, l2_s, l2_r, lc_s, lc_r, l_first)
    rest(f_buf, f2_s, f2_r, fc_s, fc_r, f_first)
    load_u.wait()
    all_logits(f_buf, f_log, fc_s, fc_r)
    rest(l_buf, l2_s, l2_r, lc_s, lc_r, l_first)
    all_logits(l_buf, l_log, lc_s, lc_r)

    place = lax.broadcasted_iota(jnp.int32, (32, 128), 1)

    def local(i, _):
        part = pl.ds(pl.multiple_of(i * 32, 32), 32)
        mean = jnp.sum(squares[part, :], axis=1, keepdims=True) / D
        inverse = lax.rsqrt(mean + EPSILON)
        inv_cols[part, :] = jnp.broadcast_to(inverse, (32, 128))
        a, b = l_log[part, :] * inverse, f_log[part, :]
        l_log[part, :] = a
        a_peak, b_peak = jnp.max(a, axis=1, keepdims=True), jnp.max(b, axis=1, keepdims=True)
        weight = jnp.exp(b - b_peak)
        found = [
            a_peak, jnp.sum(jnp.exp(a - a_peak), axis=1, keepdims=True), b_peak,
            jnp.sum(weight, axis=1, keepdims=True), jnp.sum(weight * (b - a), axis=1, keepdims=True),
        ]
        tile = jnp.zeros((32, 128), F32)
        for n, v in enumerate(found):
            tile = jnp.where(place == n, jnp.broadcast_to(v, (32, 128)), tile)
        cols[part, :] = tile
        return 0

    lax.fori_loop(0, 8, local, 0)
    st_core[7] = cols[...].T[:8]
    for j, t, _ in group:
        send(st_core.at[7], st_core.at[j], (tc_s, tc_r, (j,)), t)
    for j, _, s in group:
        recv(st_core.at[j], (tc_s, tc_r, (j,)), s)
    found = merge([st_core[j] for j in range(8)])
    for buf, n, me, at, ss, rs in ((st_x, NX, x, at_x, tx_s, tx_r), (st_z, NZ, z, at_z, tz_s, tz_r)):
        buf[n - 1] = found
        for j, t, _ in others(n, me):
            send(buf.at[n - 1], buf.at[j], (ss, rs, (j,)), at(t))
        for j, _, s in others(n, me):
            recv(buf.at[j], (ss, rs, (j,)), at(s))
        found = merge([buf[j] for j in range(n)])
    lens_total = found[0:1] + jnp.log(found[1:2])
    final_total = found[2:3] + jnp.log(found[3:4])
    apart = found[4:5] / found[3:4] + lens_total - final_total
    tall = jnp.concatenate([stack_rows([lens_total, final_total, apart]), jnp.zeros((120, 256), F32)], axis=0)
    cols[...] = tall.T
    mine = pl.ds(pl.multiple_of(half * 128 + x * 32 + quarter * 8, 8), 8)
    div[...] = jnp.broadcast_to(cols[mine, 2:3], (8, 128))

    def slopes(i, _):
        part = pl.ds(pl.multiple_of(i * 32, 32), 32)
        totals = cols[part, :]
        a = l_log[part, :]
        rounded = (jnp.exp(a - totals[:, 0:1]) - jnp.exp(f_log[part, :] - totals[:, 1:2])).astype(BF16)
        grad[part, :] = rounded
        slope = jnp.sum(rounded.astype(F32) * a, axis=1, keepdims=True)
        sl_cols[part, :] = jnp.broadcast_to(slope, (32, 128))
        return 0

    lax.fori_loop(0, 8, slopes, 0)

    def back(yy, kk):
        block = pl.ds(pl.multiple_of((yy * 2 + kk) * COLS, 128), COLS)
        return lax.dot_general(
            grad[...], u[block, :], (((1,), (1,)), ((), ())), preferred_element_type=F32
        ).reshape(2, NX, 32, COLS)

    def slope_send(buf, n, me, at, ss, rs):
        for j, t, _ in others(n, me):
            send(buf.at[n - 1], buf.at[j], (ss, rs, (j,)), at(t))

    def slope_sum(buf, n, me, at, ss, rs):
        total = buf[n - 1]
        for j, _, s in others(n, me):
            recv(buf.at[j], (ss, rs, (j,)), at(s))
            total = total + buf[j]
        return total

    over_y = (sl_y, NY, y, at_y, py_s, py_r)
    over_x = (sl_x, NX, x, at_x, px_s, px_r)
    over_z = (sl_z, NZ, z, at_z, pz_s, pz_r)
    sl_core[0] = sl_cols[...].T[:8]
    send(sl_core.at[0], sl_core.at[1], (pc_s, pc_r, ()), sibling)

    def block_y(i):
        return lax.rem(y + 1 + i, NY)

    def hand_over(i):
        return copy(c_send.at[i], c_recv.at[i], gc_s.at[i], gc_r.at[i], sibling)

    def y_far(p):
        return copy(acc.at[1, 0, pl.ds(2 * p, 2)], fy.at[p], yf_s.at[p], yf_r.at[p], at_y(block_y(2 * p)))

    def y_near(p, part):
        two = pl.ds(2 * part, 2)
        sem = (yn_s.at[p, part], yn_r.at[p, part])
        return copy(acc.at[2 * p, 0, two], ry.at[p, two], *sem, at_y(block_y(2 * p)))

    def beside(i, far):
        return lax.div(i, 2) if far else 1 - lax.div(i, 2)

    def x_at(way):
        return lax.rem(x + 1 + 2 * way, NX)

    def x_far(i):
        way = beside(i, True)
        return copy(acc.at[i, 1, lax.rem(x + 2, NX)], fx.at[i], xf_s.at[i], xf_r.at[i], at_x(x_at(way)))

    def x_near(i):
        way = beside(i, False)
        return copy(acc.at[i, 1, x_at(way)], rx.at[way, i], xn_s.at[i], xn_r.at[i], at_x(x_at(way)))

    def x_sum(i):
        way = beside(i, True)
        return copy(acc.at[i, 1, x_at(way)], rx.at[way, i], xs_s.at[i], xs_r.at[i], at_x(x_at(way)))

    def away(i):
        c_send[i] = back(block_y(i), 1 - k)
        hand_over(i).start()

    def order(i):
        return jnp.where(i < 2, 1 - i, i)

    def home(i, n):
        acc[i] = back(block_y(i), k)
        hand_over(i).wait_recv()
        acc[i] += c_recv[i]

        @pl.when(n == 0)
        def _():
            y_far(0).start()
            y_far(1).start()

        @pl.when(n == 1)
        def _():
            y_near(0, 1).start()

        @pl.when(n == 2)
        def _():
            y_near(1, 0).start()

        x_far(i).start()
        x_near(i).start()

    def both(n, _):
        @pl.when(n < NY)
        def _():
            away(order(n))

        @pl.when(n > 0)
        def _():
            home(order(n - 1), n - 1)

        return 0

    lax.fori_loop(0, NY + 1, both, 0)
    recv(sl_core.at[1], (pc_s, pc_r, ()), sibling)
    sl_y[NY - 1] = sl_core[0] + sl_core[1]
    slope_send(*over_y)
    for p in range(2):
        y_far(p).wait_recv()
        acc[2 * p, 0, 2 * p : 2 * p + 2] += fy[p]
        y_near(p, p).start()
    for i in (1, 0, 2, 3):
        x_far(i).wait_recv()
        acc[i, 1, x_at(beside(i, True))] += fx[i]
        x_sum(i).start()
    for p in range(2):
        for part in range(2):
            y_near(p, part).wait_recv()

    def add0(i, _):
        r0[i] = acc[NY - 1, 0, i] + ry[0, i] + ry[1, i]
        return 0

    lax.fori_loop(0, NX, add0, 0)
    eights = [pl.ds(8 * q, 8) for q in range(4)]
    for q, part in enumerate(eights):
        for j, t, _ in others(NX, x):
            send(r0.at[t, part], rx0.at[j, part], (g2_s, g2_r, (0, j, q)), at_x(t))
    sl_x[NX - 1] = slope_sum(*over_y)
    slope_send(*over_x)

    for i in range(NY):
        x_near(i).wait_recv()
        x_sum(i).wait_recv()
        r1[i] = acc[i, 1, x] + rx[0, i] + rx[1, i]
    for q, part in enumerate(eights):
        for i in range(NY - 1):
            send(r1.at[i, part], ry1.at[i, part], (g2_s, g2_r, (1, i, q)), at_y(block_y(i)))
    for q, part in enumerate(eights):
        for j, _, s in others(NX, x):
            recv(rx0.at[j, part], (g2_s, g2_r, (0, j, q)), at_x(s))
        sz[q] = r0[x, part] + rx0[0, part] + rx0[1, part] + rx0[2, part]
        z_send(sz, rz, gz_s, gz_r, q)
        for i in range(NY - 1):
            recv(ry1.at[i, part], (g2_s, g2_r, (1, i, q)), at_y(block_y(i)))
        sz[4 + q] = r1[NY - 1, part] + ry1[0, part] + ry1[1, part] + ry1[2, part]
        z_send(sz, rz, gz_s, gz_r, 4 + q)
    sl_z[NZ - 1] = slope_sum(*over_x)
    slope_send(*over_z)
    state_grad = sz[z]
    for j, _, s in others(NZ, z):
        recv(rz.at[j], (gz_s, gz_r, (j,)), at_z(s))
        state_grad = state_grad + rz[j]
    cols[...] = jnp.concatenate([slope_sum(*over_z), jnp.zeros((120, 256), F32)], axis=0).T
    inverse = inv_cols[mine, 0:1]
    slope = cols[mine, 0:1] / D
    delta = inverse * (gain_part * state_grad) - l_state[...] * (inverse * inverse * slope)
    sd_z[mine8] = pack(delta)
    own = sd_z.at[mine8]
    for j, t, _ in others(NZ, z):
        send(own, own, (oz_s, oz_r, (j,)), at_z(t))
    for j, t, _ in others(NX, x):
        send(own, own, (ox_s, ox_r, (0, j)), at_x(t))
    for q, _, s in others(NZ, z):
        piece = sd_z.at[slot_of(s, x)]
        recv(piece, (oz_s, oz_r, (q,)), at_z(s))
        for j, t, _ in others(NX, x):
            send(piece, piece, (ox_s, ox_r, (q + 1, j)), at_x(t))
    for q in range(NZ):
        for j, _, s in others(NX, x):
            piece = sd_z.at[slot_of(lax.rem(z + (NZ - q), NZ), s)]
            recv(piece, (ox_s, ox_r, (q, j)), at_x(s))
    found = sd_z[...].astype(F32)
    sd_out[...] = jnp.concatenate([found[:, :8], found[:, 8:, :384]], axis=2).reshape(256, COLS).astype(BF16)

    for i in range(NY):
        hand_over(i).wait_send()
        x_far(i).wait_send()
        x_near(i).wait_send()
        x_sum(i).wait_send()
    for p in range(2):
        y_far(p).wait_send()
        for part in range(2):
            y_near(p, part).wait_send()
    for _, t, _ in others(NZ, z):
        z_sum(sx, dz, d_s, d_r, t).wait_send()
        z_sum(sz, rz, gz_s, gz_r, t).wait_send()
    for one in unsent:
        one.wait_send()


def finish(rows, delta, div, gt, goff, divergence):
    gt[...] = jnp.dot(rows[...], delta[...], preferred_element_type=F32)[:ROWS]
    goff[...] = jnp.sum(delta[...].astype(F32), axis=0)
    divergence[...] = div[...].T[0]


def on_device(hidden, final_hidden, translator, offset, norm_gain, unembed):
    vm = pltpu.VMEM
    dma = pltpu.SemaphoreType.DMA
    blocks = [
        vm((8, D), BF16), vm((8, D), BF16), vm((COLS,), F32), vm((D,), BF16),
        vm((D, VOC), BF16), vm((32, 16, 128), BF16), vm((32, 16, 128), BF16), vm((256, COLS), BF16),
        vm((2, NX, 32, COLS), F32), vm((2, NX, 32, COLS), BF16), vm((3, 2, 32, COLS), BF16),
        vm((NZ, 8, COLS), F32), vm((7, 8, COLS), F32),
        vm((8, D), F32), vm((16, 512), BF16), vm((NZ, 16, 512), BF16), vm((2, NY, 2, NX, 32, COLS), BF16),
        vm((16, 512), BF16), vm((NZ, 16, 512), BF16), vm((2, NY, 2, NX, 32, COLS), BF16), vm((8, COLS), F32),
        vm((8, 8, COLS), F32), vm((8, 8, COLS), F32), vm((256, 128), F32),
        vm((256, VOC), F32), vm((256, VOC), F32),
        vm((8, 8, 256), F32), vm((NX, 8, 256), F32), vm((NZ, 8, 256), F32),
        vm((2, 8, 256), F32), vm((NY, 8, 256), F32), vm((NX, 8, 256), F32), vm((NZ, 8, 256), F32),
        vm((256, 128), F32), vm((256, 128), F32), vm((256, 128), F32), vm((256, VOC), BF16),
        vm((NY, 2, NX, 32, COLS), F32), vm((NY, 2, NX, 32, COLS), F32), vm((NY, 2, NX, 32, COLS), F32),
        vm((2, 2, 32, COLS), F32), vm((2, NX, 32, COLS), F32), vm((NY, 32, COLS), F32), vm((2, NY, 32, COLS), F32),
        vm((NX, 32, COLS), F32), vm((NY, 32, COLS), F32),
        vm((3, 32, COLS), F32), vm((3, 32, COLS), F32), vm((NZ, 8, COLS), F32), vm((7, 8, COLS), F32),
        vm((32, 16, 512), BF16),
    ]
    pairs = [
        (31,), (4, 3), (7,),
        (7,), (2, 3), (2, 4, 3), (2, 4, 4),
        (7,), (2, 3), (2, 4, 3), (2, 4, 4),
        (7,), (3,), (7,),
        (), (3,), (3,), (7,),
        (4,), (2,), (2, 2), (4,), (4,), (4,), (2, 3, 4), (7,),
        (7,), (8, 3),
    ]
    sems = [dma((6,))]
    for shape in pairs:
        sems += [dma(shape) if shape else dma] * 2
    whole = pl.BlockSpec(memory_space=pltpu.VMEM)
    rows, delta, div = pl.pallas_call(
        kernel,
        out_shape=(
            jax.ShapeDtypeStruct((256, 256), BF16),
            jax.ShapeDtypeStruct((256, COLS), BF16),
            jax.ShapeDtypeStruct((8, 128), F32),
        ),
        in_specs=[pl.BlockSpec(memory_space=pl.ANY)] * 6,
        out_specs=(whole, whole, whole),
        scratch_shapes=blocks + sems,
        compiler_params=pltpu.CompilerParams(
            collective_id=0, has_side_effects=True, vmem_limit_bytes=56 * 2**20
        ),
        name="lens_step",
    )(hidden, final_hidden, translator, offset, norm_gain, unembed)
    return pl.pallas_call(
        finish,
        out_shape=(
            jax.ShapeDtypeStruct((ROWS, COLS), F32),
            jax.ShapeDtypeStruct((COLS,), F32),
            jax.ShapeDtypeStruct((8,), F32),
        ),
        in_specs=[whole] * 3,
        out_specs=(whole, whole, whole),
        name="finish",
    )(rows, delta, div)


def solution(mesh):
    placed = (P("dp", None), P("dp", None), P("dp", "vocab"), P("vocab"), P(), P(None, ("dp", "vocab")))
    return jax.shard_map(
        on_device,
        mesh=mesh,
        in_specs=placed,
        out_specs=(P("dp", "vocab"), P("vocab"), P("dp")),
        check_vma=False,
    )
```

```python
import functools

import jax
import jax.numpy as jnp
from jax import lax
from jax.experimental import pallas as pl
from jax.experimental.pallas import tpu as pltpu
from jax.sharding import PartitionSpec as P

MESH = pl.DeviceIdType.MESH
F32, BF16 = jnp.float32, jnp.bfloat16
D = 7168
COLS = 896
ROWS = 224
VOC = 512
EPSILON = 1e-06
NZ, NX, NY = 8, 4, 4


def pack(a):
    low = jnp.concatenate([a[:, 512:], jnp.zeros((8, 128), F32)], axis=1)
    return jnp.concatenate([a[:, :512], low], axis=0).astype(BF16)


def unpack(blocks):
    wide = blocks.astype(F32)
    return jnp.concatenate([wide[:, :8], wide[:, 8:, :384]], axis=2).reshape(64, COLS).astype(BF16)


def merge(tiles):
    lens_peak = functools.reduce(jnp.maximum, [t[0:1] for t in tiles])
    final_peak = functools.reduce(jnp.maximum, [t[2:3] for t in tiles])
    lens_sum = sum(t[1:2] * jnp.exp(t[0:1] - lens_peak) for t in tiles)
    scales = [jnp.exp(t[2:3] - final_peak) for t in tiles]
    final_sum = sum(t[3:4] * s for t, s in zip(tiles, scales))
    cross = sum(t[4:5] * s for t, s in zip(tiles, scales))
    return stack_rows([lens_peak, lens_sum, final_peak, final_sum, cross])


def stack_rows(rows):
    place = lax.broadcasted_iota(jnp.int32, (8, 256), 0)
    tile = jnp.zeros((8, 256), F32)
    for i, row in enumerate(rows):
        tile = jnp.where(place == i, jnp.broadcast_to(row, (8, 256)), tile)
    return tile


def kernel(
    hid_in, fin_in, tw_in, off_in, gain_in, unemb, rows_out, sd_out, div,
    hid, fin, off, gain, u, hpack, hin, twp, mapped, mapped_b, cx, sx, dz,
    f_norm, f_pack, f_z, f_buf, l_pack, l_z, l_buf, l_state, gains, regain, squares,
    l_log, f_log, st_core, st_x, st_z, sl_core, sl_y, sl_x, sl_z, cols, inv_cols, sl_cols, grad,
    c_send, c_recv, acc, fy, ry, fx, rx, r0, r1, rx0, ry1, sz, rz,
    sd_z,
    in_sem, a_s, a_r, c_s, c_r, d_s, d_r,
    fz_s, fz_r, f1_s, f1_r, f2_s, f2_r, fc_s, fc_r,
    lz_s, lz_r, l1_s, l1_r, l2_s, l2_r, lc_s, lc_r,
    tc_s, tc_r, tx_s, tx_r, tz_s, tz_r,
    pc_s, pc_r, py_s, py_r, px_s, px_r, pz_s, pz_r,
    gc_s, gc_r, yf_s, yf_r, yn_s, yn_r, xf_s, xf_r, xn_s, xn_r, xs_s, xs_r, g2_s, g2_r, gz_s, gz_r,
    oz_s, oz_r, ox_s, ox_r,
):
    r, c = lax.axis_index("dp"), lax.axis_index("vocab")
    z, x = lax.div(r, NX), lax.rem(r, NX)
    y, k = lax.div(c, 2), lax.rem(c, 2)
    half, quarter = lax.div(z, 4), lax.rem(z, 4)
    feat = pl.ds(pl.multiple_of(c * COLS, 128), COLS)

    def at_z(i):
        return (i * NX + x, c)

    def at_x(i):
        return (z * NX + i, c)

    def at_y(i):
        return (r, i * 2 + k)

    sibling = (r, y * 2 + (1 - k))
    unsent = []

    def copy(src, dst, ss, rs, dev):
        return pltpu.make_async_remote_copy(
            src_ref=src, dst_ref=dst, send_sem=ss, recv_sem=rs, device_id=dev, device_id_type=MESH
        )

    def pair(sem):
        ss, rs, at = sem
        return (ss.at[at], rs.at[at]) if at else (ss, rs)

    def send(src, dst, sem, dev):
        one = copy(src, dst, *pair(sem), dev)
        one.start()
        unsent.append(one)

    def recv(land, sem, dev):
        copy(land, land, *pair(sem), dev).wait_recv()

    def others(n, me):
        far_first = sorted(range(1, n), key=lambda d: -min(d, n - d))
        return [(d - 1, lax.rem(me + d, n), lax.rem(me + (n - d), n)) for d in far_first]

    rings = {id(me): others(n, me) for n, me in ((NZ, z), (NX, x), (NY, y))}

    def others(n, me):
        return rings[id(me)]

    barrier = pltpu.get_barrier_semaphore()
    def slot_of(i, j):
        return lax.div(i, 4) * 16 + j * 4 + lax.rem(i, 4)

    steps = [(i, j) for i in range(NZ) for j in range(NX) if i + j]
    steps.sort(key=lambda s: -(min(s[0], NZ - s[0]) + min(s[1], NX - s[1])))
    plane = []
    for i, j in steps:
        ahead = (lax.rem(z + i, NZ), lax.rem(x + j, NX))
        behind = (lax.rem(z + (NZ - i), NZ), lax.rem(x + (NX - j), NX))
        plane.append((len(plane), ahead, behind))
    partners = [(zz * NX + xx, c) for _, (zz, xx), _ in plane]
    group = [(d - 1, (r, lax.rem(c + d, 8)), (r, lax.rem(c + (8 - d), 8))) for d in range(1, 8)]
    partners += [t for _, t, _ in group]
    for p in partners:
        pl.semaphore_signal(barrier, inc=1, device_id=p, device_id_type=MESH)
    pairs = [(hid_in, hid), (fin_in, fin), (gain_in, gain), (tw_in, twp.at[pl.ds(0, ROWS)]), (off_in, off), (unemb, u)]
    loads = [pltpu.make_async_copy(src, dst, in_sem.at[i]) for i, (src, dst) in enumerate(pairs)]
    load_hid, load_fin, load_gain, load_tw, load_off, load_u = loads
    for load in loads:
        load.start()
    load_hid.wait()

    flat = hid[...].astype(F32)
    for i in range(NZ * NX):
        low = jnp.concatenate([flat[:, i * ROWS + 128 : (i + 1) * ROWS], jnp.zeros((8, 32), F32)], axis=1)
        hpack[i] = jnp.concatenate([flat[:, i * ROWS : i * ROWS + 128], low], axis=0).astype(BF16)
    pl.semaphore_wait(barrier, len(partners))

    mine8 = slot_of(z, x)
    for j, (zz, xx), _ in plane:
        send(hpack.at[zz * NX + xx], hin.at[mine8], (a_s, a_r, (j,)), (zz * NX + xx, c))
    hin[mine8] = hpack[r]
    load_fin.wait()
    load_gain.wait()
    wide = fin[...].astype(F32)
    final_inverse = lax.rsqrt(jnp.sum(wide * wide, axis=1, keepdims=True) / D + EPSILON)
    gain_all = gain[...].astype(F32).reshape(1, D)
    f_norm[...] = wide * final_inverse * gain_all
    f_pack[...] = pack(f_norm[:, feat])
    for i in range(8):
        gains[i] = jnp.broadcast_to(gain_all[:, i * COLS : (i + 1) * COLS], (8, COLS))
        regain[i] = 1.0 / gains[i]
    twp[ROWS:] = jnp.zeros((256 - ROWS, COLS), BF16)
    for j, t, _ in others(NZ, z):
        send(f_pack, f_z.at[z], (fz_s, fz_r, (j,)), at_z(t))
    f_z[z] = f_pack[...]

    def own_pieces(buf, flat, s1, r1, s2, r2):
        for h in range(2):
            buf[k, y, h, x] = flat[h * 32 : (h + 1) * 32]
        for stage in range(2):
            for h in range(2):
                piece = buf.at[k, y, h, x]
                along_x = h == stage
                n, me, at = (NX, x, at_x) if along_x else (NY, y, at_y)
                for j, t, _ in others(n, me):
                    sem = (s1, r1, (h, j)) if stage == 0 else (s2, r2, (h, 0, j))
                    send(piece, piece, sem, at(t))
    def to_sibling(buf, yy, h, sc, rc, q):
        block = buf.at[k, yy, h]
        send(block, block, (sc, rc, (h, q)), sibling)

    def forward(buf, s1, r1, s2, r2, sc, rc):
        for q in (1, 3, 2):
            for h in range(2):
                if h == 0:
                    s = lax.rem(x + (NX - q), NX)
                    piece, dev, n2, m2, at2 = buf.at[k, y, h, s], at_x(s), NY, y, at_y
                else:
                    s = lax.rem(y + (NY - q), NY)
                    piece, dev, n2, m2, at2 = buf.at[k, s, h, x], at_y(s), NX, x, at_x
                recv(piece, (s1, r1, (h, q - 1)), dev)
                for j, t, _ in others(n2, m2):
                    send(piece, piece, (s2, r2, (h, q, j)), at2(t))
        to_sibling(buf, y, 0, sc, rc, 0)

    def rest(buf, s2, r2, sc, rc):
        def half0(q):
            yy = lax.rem(y + (NY - q), NY)
            for j in range(NX):
                xx = lax.rem(x + (NX - j), NX)
                recv(buf.at[k, yy, 0, xx], (s2, r2, (0, j, q - 1)), at_y(yy))
            to_sibling(buf, yy, 0, sc, rc, q)

        def half1(j):
            yy = lax.rem(y + (NY - j), NY)
            for q in (1, 3, 2):
                xx = lax.rem(x + (NX - q), NX)
                recv(buf.at[k, yy, 1, xx], (s2, r2, (1, j, q - 1)), at_x(xx))
            to_sibling(buf, yy, 1, sc, rc, j)

        half1(0)
        half0(1)
        half1(1)
        half0(3)
        half1(3)
        half0(2)
        half1(2)

    def all_logits(buf, log, sc, rc):
        def step(n, _):
            q = lax.rem(n, NY)
            yy, kk = lax.rem(y + (NY - q), NY), jnp.where(n < NY, k, 1 - k)

            @pl.when(n >= NY)
            def _():
                for h in range(2):
                    recv(buf.at[1 - k, yy, h], (sc, rc, (h, q)), sibling)

            cc = yy * 2 + kk
            block = pl.ds(pl.multiple_of(cc * COLS, 128), COLS)
            value = buf[kk, yy].reshape(256, COLS)
            log[...] += jnp.dot(value, u[block, :], preferred_element_type=F32)
            if buf is l_buf:
                scale = regain[cc][0:1]
                total = squares[...]
                for i in range(COLS // 128):
                    lanes = slice(i * 128, (i + 1) * 128)
                    plain = value[:, lanes].astype(F32) * scale[:, lanes]
                    total = total + plain * plain
                squares[...] = total
            return 0

        lax.fori_loop(0, 8, step, 0)

    for j, _, (zz, xx) in plane:
        recv(hin.at[slot_of(zz, xx)], (a_s, a_r, (j,)), (zz * NX + xx, c))
    found = hin[...].astype(F32)
    load_tw.wait()
    rows = jnp.concatenate([found[:, :8].reshape(256, 128), found[:, 8:].reshape(256, 128)], axis=1)
    product = jnp.dot(rows.astype(BF16), twp[...], preferred_element_type=F32)
    mapped[...] = product.reshape(2, NX, 32, COLS)
    mapped_b[...] = product.astype(BF16).reshape(2, NX, 32, COLS)
    quarters = [(h, pl.ds(16 * p, 16)) for h in range(2) for p in range(2)]
    for p, (h, part) in enumerate(quarters):
        for j, t, _ in others(NX, x):
            send(mapped_b.at[h, t, part], cx.at[j, h, part], (c_s, c_r, (p, j)), at_x(t))

    def z_sum(src, dst, ss, rs, zz):
        place = lax.rem(zz - z + NZ, NZ) - 1
        return copy(src.at[zz], dst.at[place], ss.at[place], rs.at[place], at_z(zz))

    def z_send(src, dst, ss, rs, zz):
        @pl.when(z != zz)
        def _():
            z_sum(src, dst, ss, rs, zz).start()

    for j, _, s in others(NZ, z):
        recv(f_z.at[s], (fz_s, fz_r, (j,)), at_z(s))
    own_pieces(f_buf, unpack(f_z[...]), f1_s, f1_r, f2_s, f2_r)
    rows_out[...] = rows.T.astype(BF16)
    for p, (h, part) in enumerate(quarters):
        for j, _, s in others(NX, x):
            recv(cx.at[j, h, part], (c_s, c_r, (p, j)), at_x(s))
        total = mapped[h, x, part]
        for j in range(3):
            total = total + cx[j, h, part].astype(F32)
        sx[2 * p : 2 * p + 2] = total.reshape(2, 8, COLS)
        z_send(sx, dz, d_s, d_r, 2 * p)
        z_send(sx, dz, d_s, d_r, 2 * p + 1)
    load_off.wait()
    forward(f_buf, f1_s, f1_r, f2_s, f2_r, fc_s, fc_r)
    base = hid[:, feat].astype(F32) + off[...].reshape(1, COLS) + sx[z]
    gain_part = gains[c]
    for j, _, s in others(NZ, z):
        recv(dz.at[j], (d_s, d_r, (j,)), at_z(s))
        base = base + dz[j]
    l_state[...] = base

    l_pack[...] = pack(base * gain_part)
    for j, t, _ in others(NZ, z):
        send(l_pack, l_z.at[z], (lz_s, lz_r, (j,)), at_z(t))
    l_z[z] = l_pack[...]
    squares[...] = jnp.zeros_like(squares)
    l_log[...] = jnp.zeros_like(l_log)
    f_log[...] = jnp.zeros_like(f_log)
    for j, _, s in others(NZ, z):
        recv(l_z.at[s], (lz_s, lz_r, (j,)), at_z(s))
    own_pieces(l_buf, unpack(l_z[...]), l1_s, l1_r, l2_s, l2_r)
    forward(l_buf, l1_s, l1_r, l2_s, l2_r, lc_s, lc_r)
    rest(f_buf, f2_s, f2_r, fc_s, fc_r)
    load_u.wait()
    all_logits(f_buf, f_log, fc_s, fc_r)
    rest(l_buf, l2_s, l2_r, lc_s, lc_r)
    all_logits(l_buf, l_log, lc_s, lc_r)

    place = lax.broadcasted_iota(jnp.int32, (32, 128), 1)

    def local(i, _):
        part = pl.ds(pl.multiple_of(i * 32, 32), 32)
        mean = jnp.sum(squares[part, :], axis=1, keepdims=True) / D
        inverse = lax.rsqrt(mean + EPSILON)
        inv_cols[part, :] = jnp.broadcast_to(inverse, (32, 128))
        a, b = l_log[part, :] * inverse, f_log[part, :]
        l_log[part, :] = a
        a_peak, b_peak = jnp.max(a, axis=1, keepdims=True), jnp.max(b, axis=1, keepdims=True)
        weight = jnp.exp(b - b_peak)
        found = [
            a_peak, jnp.sum(jnp.exp(a - a_peak), axis=1, keepdims=True), b_peak,
            jnp.sum(weight, axis=1, keepdims=True), jnp.sum(weight * (b - a), axis=1, keepdims=True),
        ]
        tile = jnp.zeros((32, 128), F32)
        for n, v in enumerate(found):
            tile = jnp.where(place == n, jnp.broadcast_to(v, (32, 128)), tile)
        cols[part, :] = tile
        return 0

    lax.fori_loop(0, 8, local, 0)
    st_core[7] = cols[...].T[:8]
    for j, t, _ in group:
        send(st_core.at[7], st_core.at[j], (tc_s, tc_r, (j,)), t)
    for j, _, s in group:
        recv(st_core.at[j], (tc_s, tc_r, (j,)), s)
    found = merge([st_core[j] for j in range(8)])
    for buf, n, me, at, ss, rs in ((st_x, NX, x, at_x, tx_s, tx_r), (st_z, NZ, z, at_z, tz_s, tz_r)):
        buf[n - 1] = found
        for j, t, _ in others(n, me):
            send(buf.at[n - 1], buf.at[j], (ss, rs, (j,)), at(t))
        for j, _, s in others(n, me):
            recv(buf.at[j], (ss, rs, (j,)), at(s))
        found = merge([buf[j] for j in range(n)])
    lens_total = found[0:1] + jnp.log(found[1:2])
    final_total = found[2:3] + jnp.log(found[3:4])
    apart = found[4:5] / found[3:4] + lens_total - final_total
    tall = jnp.concatenate([stack_rows([lens_total, final_total, apart]), jnp.zeros((120, 256), F32)], axis=0)
    cols[...] = tall.T
    mine = pl.ds(pl.multiple_of(half * 128 + x * 32 + quarter * 8, 8), 8)
    div[...] = jnp.broadcast_to(cols[mine, 2:3], (8, 128))

    def slopes(i, _):
        part = pl.ds(pl.multiple_of(i * 32, 32), 32)
        totals = cols[part, :]
        a = l_log[part, :]
        rounded = (jnp.exp(a - totals[:, 0:1]) - jnp.exp(f_log[part, :] - totals[:, 1:2])).astype(BF16)
        grad[part, :] = rounded
        slope = jnp.sum(rounded.astype(F32) * a, axis=1, keepdims=True)
        sl_cols[part, :] = jnp.broadcast_to(slope, (32, 128))
        return 0

    lax.fori_loop(0, 8, slopes, 0)

    def back(yy, kk):
        block = pl.ds(pl.multiple_of((yy * 2 + kk) * COLS, 128), COLS)
        return lax.dot_general(
            grad[...], u[block, :], (((1,), (1,)), ((), ())), preferred_element_type=F32
        ).reshape(2, NX, 32, COLS)

    def slope_send(buf, n, me, at, ss, rs):
        for j, t, _ in others(n, me):
            send(buf.at[n - 1], buf.at[j], (ss, rs, (j,)), at(t))

    def slope_sum(buf, n, me, at, ss, rs):
        total = buf[n - 1]
        for j, _, s in others(n, me):
            recv(buf.at[j], (ss, rs, (j,)), at(s))
            total = total + buf[j]
        return total

    over_y = (sl_y, NY, y, at_y, py_s, py_r)
    over_x = (sl_x, NX, x, at_x, px_s, px_r)
    over_z = (sl_z, NZ, z, at_z, pz_s, pz_r)
    sl_core[0] = sl_cols[...].T[:8]
    send(sl_core.at[0], sl_core.at[1], (pc_s, pc_r, ()), sibling)

    def block_y(i):
        return lax.rem(y + 1 + i, NY)

    def hand_over(i):
        return copy(c_send.at[i], c_recv.at[i], gc_s.at[i], gc_r.at[i], sibling)

    def y_far(p):
        return copy(acc.at[1, 0, pl.ds(2 * p, 2)], fy.at[p], yf_s.at[p], yf_r.at[p], at_y(block_y(2 * p)))

    def y_near(p, part):
        two = pl.ds(2 * part, 2)
        sem = (yn_s.at[p, part], yn_r.at[p, part])
        return copy(acc.at[2 * p, 0, two], ry.at[p, two], *sem, at_y(block_y(2 * p)))

    def beside(i, far):
        return lax.div(i, 2) if far else 1 - lax.div(i, 2)

    def x_at(way):
        return lax.rem(x + 1 + 2 * way, NX)

    def x_far(i):
        way = beside(i, True)
        return copy(acc.at[i, 1, lax.rem(x + 2, NX)], fx.at[i], xf_s.at[i], xf_r.at[i], at_x(x_at(way)))

    def x_near(i):
        way = beside(i, False)
        return copy(acc.at[i, 1, x_at(way)], rx.at[way, i], xn_s.at[i], xn_r.at[i], at_x(x_at(way)))

    def x_sum(i):
        way = beside(i, True)
        return copy(acc.at[i, 1, x_at(way)], rx.at[way, i], xs_s.at[i], xs_r.at[i], at_x(x_at(way)))

    def away(i):
        c_send[i] = back(block_y(i), 1 - k)
        hand_over(i).start()

    def order(i):
        return jnp.where(i < 2, 1 - i, i)

    def home(i, n):
        acc[i] = back(block_y(i), k)
        hand_over(i).wait_recv()
        acc[i] += c_recv[i]

        @pl.when(n == 0)
        def _():
            y_far(0).start()
            y_far(1).start()

        @pl.when(n == 1)
        def _():
            y_near(0, 1).start()

        @pl.when(n == 2)
        def _():
            y_near(1, 0).start()

        x_far(i).start()
        x_near(i).start()

    def both(n, _):
        @pl.when(n < NY)
        def _():
            away(order(n))

        @pl.when(n > 0)
        def _():
            home(order(n - 1), n - 1)

        return 0

    lax.fori_loop(0, NY + 1, both, 0)
    recv(sl_core.at[1], (pc_s, pc_r, ()), sibling)
    sl_y[NY - 1] = sl_core[0] + sl_core[1]
    slope_send(*over_y)
    for p in range(2):
        y_far(p).wait_recv()
        acc[2 * p, 0, 2 * p : 2 * p + 2] += fy[p]
        y_near(p, p).start()
    for i in (1, 0, 2, 3):
        x_far(i).wait_recv()
        acc[i, 1, x_at(beside(i, True))] += fx[i]
        x_sum(i).start()
    for p in range(2):
        for part in range(2):
            y_near(p, part).wait_recv()

    def add0(i, _):
        r0[i] = acc[NY - 1, 0, i] + ry[0, i] + ry[1, i]
        return 0

    lax.fori_loop(0, NX, add0, 0)
    eights = [pl.ds(8 * q, 8) for q in range(4)]
    for q, part in enumerate(eights):
        for j, t, _ in others(NX, x):
            send(r0.at[t, part], rx0.at[j, part], (g2_s, g2_r, (0, j, q)), at_x(t))
    sl_x[NX - 1] = slope_sum(*over_y)
    slope_send(*over_x)

    for i in range(NY):
        x_near(i).wait_recv()
        x_sum(i).wait_recv()
        r1[i] = acc[i, 1, x] + rx[0, i] + rx[1, i]
    for q, part in enumerate(eights):
        for i in range(NY - 1):
            send(r1.at[i, part], ry1.at[i, part], (g2_s, g2_r, (1, i, q)), at_y(block_y(i)))
    for q, part in enumerate(eights):
        for j, _, s in others(NX, x):
            recv(rx0.at[j, part], (g2_s, g2_r, (0, j, q)), at_x(s))
        sz[q] = r0[x, part] + rx0[0, part] + rx0[1, part] + rx0[2, part]
        z_send(sz, rz, gz_s, gz_r, q)
        for i in range(NY - 1):
            recv(ry1.at[i, part], (g2_s, g2_r, (1, i, q)), at_y(block_y(i)))
        sz[4 + q] = r1[NY - 1, part] + ry1[0, part] + ry1[1, part] + ry1[2, part]
        z_send(sz, rz, gz_s, gz_r, 4 + q)
    sl_z[NZ - 1] = slope_sum(*over_x)
    slope_send(*over_z)
    state_grad = sz[z]
    for j, _, s in others(NZ, z):
        recv(rz.at[j], (gz_s, gz_r, (j,)), at_z(s))
        state_grad = state_grad + rz[j]
    cols[...] = jnp.concatenate([slope_sum(*over_z), jnp.zeros((120, 256), F32)], axis=0).T
    inverse = inv_cols[mine, 0:1]
    slope = cols[mine, 0:1] / D
    delta = inverse * (gain_part * state_grad) - l_state[...] * (inverse * inverse * slope)
    sd_z[mine8] = pack(delta)
    own = sd_z.at[mine8]
    for j, t, _ in others(NZ, z):
        send(own, own, (oz_s, oz_r, (j,)), at_z(t))

    def four(hh, xx):
        return sd_z.at[pl.ds(hh * 16 + xx * 4, 4)]

    for near in range(2):
        hh = half if near == 0 else 1 - half
        for i in range(4):
            s = hh * 4 + i

            @pl.when(s != z)
            def _():
                place = lax.rem(z - s + NZ, NZ) - 1
                piece = sd_z.at[slot_of(s, x)]
                copy(piece, piece, oz_s.at[place], oz_r.at[place], at_z(s)).wait_recv()

        for j, t, _ in others(NX, x):
            send(four(hh, x), four(hh, x), (ox_s, ox_r, (near, j)), at_x(t))
    for near in range(2):
        hh = half if near == 0 else 1 - half
        for j, _, s in others(NX, x):
            recv(four(hh, s), (ox_s, ox_r, (near, j)), at_x(s))
    found = sd_z[...].astype(F32)
    sd_out[...] = jnp.concatenate([found[:, :8], found[:, 8:, :384]], axis=2).reshape(256, COLS).astype(BF16)

    for i in range(NY):
        hand_over(i).wait_send()
        x_far(i).wait_send()
        x_near(i).wait_send()
        x_sum(i).wait_send()
    for p in range(2):
        y_far(p).wait_send()
        for part in range(2):
            y_near(p, part).wait_send()
    for _, t, _ in others(NZ, z):
        z_sum(sx, dz, d_s, d_r, t).wait_send()
        z_sum(sz, rz, gz_s, gz_r, t).wait_send()
    for one in unsent:
        one.wait_send()


def finish(rows, delta, div, gt, goff, divergence):
    gt[...] = jnp.dot(rows[...], delta[...], preferred_element_type=F32)[:ROWS]
    goff[...] = jnp.sum(delta[...].astype(F32), axis=0)
    divergence[...] = div[...].T[0]


def on_device(hidden, final_hidden, translator, offset, norm_gain, unembed):
    vm = pltpu.VMEM
    dma = pltpu.SemaphoreType.DMA
    blocks = [
        vm((8, D), BF16), vm((8, D), BF16), vm((COLS,), F32), vm((D,), BF16),
        vm((D, VOC), BF16), vm((32, 16, 128), BF16), vm((32, 16, 128), BF16), vm((256, COLS), BF16),
        vm((2, NX, 32, COLS), F32), vm((2, NX, 32, COLS), BF16), vm((3, 2, 32, COLS), BF16),
        vm((NZ, 8, COLS), F32), vm((7, 8, COLS), F32),
        vm((8, D), F32), vm((16, 512), BF16), vm((NZ, 16, 512), BF16), vm((2, NY, 2, NX, 32, COLS), BF16),
        vm((16, 512), BF16), vm((NZ, 16, 512), BF16), vm((2, NY, 2, NX, 32, COLS), BF16), vm((8, COLS), F32),
        vm((8, 8, COLS), F32), vm((8, 8, COLS), F32), vm((256, 128), F32),
        vm((256, VOC), F32), vm((256, VOC), F32),
        vm((8, 8, 256), F32), vm((NX, 8, 256), F32), vm((NZ, 8, 256), F32),
        vm((2, 8, 256), F32), vm((NY, 8, 256), F32), vm((NX, 8, 256), F32), vm((NZ, 8, 256), F32),
        vm((256, 128), F32), vm((256, 128), F32), vm((256, 128), F32), vm((256, VOC), BF16),
        vm((NY, 2, NX, 32, COLS), F32), vm((NY, 2, NX, 32, COLS), F32), vm((NY, 2, NX, 32, COLS), F32),
        vm((2, 2, 32, COLS), F32), vm((2, NX, 32, COLS), F32), vm((NY, 32, COLS), F32), vm((2, NY, 32, COLS), F32),
        vm((NX, 32, COLS), F32), vm((NY, 32, COLS), F32),
        vm((3, 32, COLS), F32), vm((3, 32, COLS), F32), vm((NZ, 8, COLS), F32), vm((7, 8, COLS), F32),
        vm((32, 16, 512), BF16),
    ]
    pairs = [
        (31,), (4, 3), (7,),
        (7,), (2, 3), (2, 4, 3), (2, 4),
        (7,), (2, 3), (2, 4, 3), (2, 4),
        (7,), (3,), (7,),
        (), (3,), (3,), (7,),
        (4,), (2,), (2, 2), (4,), (4,), (4,), (2, 3, 4), (7,),
        (7,), (2, 3),
    ]
    sems = [dma((6,))]
    for shape in pairs:
        sems += [dma(shape) if shape else dma] * 2
    whole = pl.BlockSpec(memory_space=pltpu.VMEM)
    rows, delta, div = pl.pallas_call(
        kernel,
        out_shape=(
            jax.ShapeDtypeStruct((256, 256), BF16),
            jax.ShapeDtypeStruct((256, COLS), BF16),
            jax.ShapeDtypeStruct((8, 128), F32),
        ),
        in_specs=[pl.BlockSpec(memory_space=pl.ANY)] * 6,
        out_specs=(whole, whole, whole),
        scratch_shapes=blocks + sems,
        compiler_params=pltpu.CompilerParams(
            collective_id=0, has_side_effects=True, vmem_limit_bytes=56 * 2**20
        ),
        name="lens_step",
    )(hidden, final_hidden, translator, offset, norm_gain, unembed)
    return pl.pallas_call(
        finish,
        out_shape=(
            jax.ShapeDtypeStruct((ROWS, COLS), F32),
            jax.ShapeDtypeStruct((COLS,), F32),
            jax.ShapeDtypeStruct((8,), F32),
        ),
        in_specs=[whole] * 3,
        out_specs=(whole, whole, whole),
        name="finish",
    )(rows, delta, div)


def solution(mesh):
    placed = (P("dp", None), P("dp", None), P("dp", "vocab"), P("vocab"), P(), P(None, ("dp", "vocab")))
    return jax.shard_map(
        on_device,
        mesh=mesh,
        in_specs=placed,
        out_specs=(P("dp", "vocab"), P("vocab"), P("dp")),
        check_vma=False,
    )
```

```python
import functools

import jax
import jax.numpy as jnp
from jax import lax
from jax.experimental import pallas as pl
from jax.experimental.pallas import tpu as pltpu
from jax.sharding import PartitionSpec as P

MESH = pl.DeviceIdType.MESH
F32, BF16 = jnp.float32, jnp.bfloat16
D = 7168
COLS = 896
ROWS = 224
VOC = 512
EPSILON = 1e-06
NZ, NX, NY = 8, 4, 4


def pack(a):
    low = jnp.concatenate([a[:, 512:], jnp.zeros((8, 128), F32)], axis=1)
    return jnp.concatenate([a[:, :512], low], axis=0).astype(BF16)


def unpack(blocks):
    wide = blocks.astype(F32)
    return jnp.concatenate([wide[:, :8], wide[:, 8:, :384]], axis=2).reshape(64, COLS).astype(BF16)


def merge(tiles):
    lens_peak = functools.reduce(jnp.maximum, [t[0:1] for t in tiles])
    final_peak = functools.reduce(jnp.maximum, [t[2:3] for t in tiles])
    lens_sum = sum(t[1:2] * jnp.exp(t[0:1] - lens_peak) for t in tiles)
    scales = [jnp.exp(t[2:3] - final_peak) for t in tiles]
    final_sum = sum(t[3:4] * s for t, s in zip(tiles, scales))
    cross = sum(t[4:5] * s for t, s in zip(tiles, scales))
    return stack_rows([lens_peak, lens_sum, final_peak, final_sum, cross])


def stack_rows(rows):
    place = lax.broadcasted_iota(jnp.int32, (8, 256), 0)
    tile = jnp.zeros((8, 256), F32)
    for i, row in enumerate(rows):
        tile = jnp.where(place == i, jnp.broadcast_to(row, (8, 256)), tile)
    return tile


def kernel(
    hid_in, fin_in, tw_in, off_in, gain_in, unemb, rows_out, sd_out, div,
    hid, fin, off, gain, u, hpack, hin, twp, mapped, mapped_b, cx, sx, dz,
    f_norm, f_pack, f_z, f_buf, l_pack, l_z, l_buf, l_state, gains, regain, squares,
    l_log, f_log, st_core, st_x, st_z, sl_core, sl_y, sl_x, sl_z, cols, inv_cols, sl_cols, grad,
    c_send, c_recv, acc, fy, ry, fx, rx, r0, r1, rx0, ry1, sz, rz,
    sd_z,
    in_sem, a_s, a_r, c_s, c_r, d_s, d_r,
    fz_s, fz_r, f1_s, f1_r, f2_s, f2_r, fc_s, fc_r,
    lz_s, lz_r, l1_s, l1_r, l2_s, l2_r, lc_s, lc_r,
    tc_s, tc_r, tx_s, tx_r, tz_s, tz_r,
    pc_s, pc_r, py_s, py_r, px_s, px_r, pz_s, pz_r,
    gc_s, gc_r, yf_s, yf_r, yn_s, yn_r, xf_s, xf_r, xn_s, xn_r, xs_s, xs_r, g2_s, g2_r, gz_s, gz_r,
    oz_s, oz_r, ox_s, ox_r,
):
    r, c = lax.axis_index("dp"), lax.axis_index("vocab")
    z, x = lax.div(r, NX), lax.rem(r, NX)
    y, k = lax.div(c, 2), lax.rem(c, 2)
    half, quarter = lax.div(z, 4), lax.rem(z, 4)
    feat = pl.ds(pl.multiple_of(c * COLS, 128), COLS)

    def at_z(i):
        return (i * NX + x, c)

    def at_x(i):
        return (z * NX + i, c)

    def at_y(i):
        return (r, i * 2 + k)

    sibling = (r, y * 2 + (1 - k))
    unsent = []

    def copy(src, dst, ss, rs, dev):
        return pltpu.make_async_remote_copy(
            src_ref=src, dst_ref=dst, send_sem=ss, recv_sem=rs, device_id=dev, device_id_type=MESH
        )

    def pair(sem):
        ss, rs, at = sem
        return (ss.at[at], rs.at[at]) if at else (ss, rs)

    def send(src, dst, sem, dev):
        one = copy(src, dst, *pair(sem), dev)
        one.start()
        unsent.append(one)

    def recv(land, sem, dev):
        copy(land, land, *pair(sem), dev).wait_recv()

    def others(n, me):
        far_first = sorted(range(1, n), key=lambda d: -min(d, n - d))
        return [(d - 1, lax.rem(me + d, n), lax.rem(me + (n - d), n)) for d in far_first]

    rings = {id(me): others(n, me) for n, me in ((NZ, z), (NX, x), (NY, y))}

    def others(n, me):
        return rings[id(me)]

    barrier = pltpu.get_barrier_semaphore()
    def slot_of(i, j):
        return lax.div(i, 4) * 16 + j * 4 + lax.rem(i, 4)

    steps = [(i, j) for i in range(NZ) for j in range(NX) if i + j]
    steps.sort(key=lambda s: -(min(s[0], NZ - s[0]) + min(s[1], NX - s[1])))
    plane = []
    for i, j in steps:
        ahead = (lax.rem(z + i, NZ), lax.rem(x + j, NX))
        behind = (lax.rem(z + (NZ - i), NZ), lax.rem(x + (NX - j), NX))
        plane.append((len(plane), ahead, behind))
    partners = [(zz * NX + xx, c) for _, (zz, xx), _ in plane]
    group = [(d - 1, (r, lax.rem(c + d, 8)), (r, lax.rem(c + (8 - d), 8))) for d in (4, 3, 5, 2, 6, 1, 7)]
    partners += [t for _, t, _ in group]
    for p in partners:
        pl.semaphore_signal(barrier, inc=1, device_id=p, device_id_type=MESH)
    pairs = [(hid_in, hid), (fin_in, fin), (gain_in, gain), (tw_in, twp.at[pl.ds(0, ROWS)]), (off_in, off), (unemb, u)]
    loads = [pltpu.make_async_copy(src, dst, in_sem.at[i]) for i, (src, dst) in enumerate(pairs)]
    load_hid, load_fin, load_gain, load_tw, load_off, load_u = loads
    for load in loads:
        load.start()
    load_hid.wait()

    flat = hid[...].astype(F32)
    for i in range(NZ * NX):
        low = jnp.concatenate([flat[:, i * ROWS + 128 : (i + 1) * ROWS], jnp.zeros((8, 32), F32)], axis=1)
        hpack[i] = jnp.concatenate([flat[:, i * ROWS : i * ROWS + 128], low], axis=0).astype(BF16)
    pl.semaphore_wait(barrier, len(partners))

    mine8 = slot_of(z, x)
    for j, (zz, xx), _ in plane:
        send(hpack.at[zz * NX + xx], hin.at[mine8], (a_s, a_r, (j,)), (zz * NX + xx, c))
    hin[mine8] = hpack[r]
    load_fin.wait()
    load_gain.wait()
    wide = fin[...].astype(F32)
    final_inverse = lax.rsqrt(jnp.sum(wide * wide, axis=1, keepdims=True) / D + EPSILON)
    gain_all = gain[...].astype(F32).reshape(1, D)
    f_norm[...] = wide * final_inverse * gain_all
    f_pack[...] = pack(f_norm[:, feat])
    for i in range(8):
        gains[i] = jnp.broadcast_to(gain_all[:, i * COLS : (i + 1) * COLS], (8, COLS))
        regain[i] = 1.0 / gains[i]
    twp[ROWS:] = jnp.zeros((256 - ROWS, COLS), BF16)
    for j, t, _ in others(NZ, z):
        send(f_pack, f_z.at[z], (fz_s, fz_r, (j,)), at_z(t))
    f_z[z] = f_pack[...]

    def own_pieces(buf, flat, s1, r1, s2, r2):
        for h in range(2):
            buf[k, y, h, x] = flat[h * 32 : (h + 1) * 32]
        for stage in range(2):
            for h in range(2):
                piece = buf.at[k, y, h, x]
                along_x = h == stage
                n, me, at = (NX, x, at_x) if along_x else (NY, y, at_y)
                for j, t, _ in others(n, me):
                    sem = (s1, r1, (h, j)) if stage == 0 else (s2, r2, (h, 0, j))
                    send(piece, piece, sem, at(t))
    def to_sibling(buf, yy, h, sc, rc, q):
        block = buf.at[k, yy, h]
        send(block, block, (sc, rc, (h, q)), sibling)

    def forward(buf, s1, r1, s2, r2, sc, rc):
        for q in (1, 3, 2):
            for h in range(2):
                if h == 0:
                    s = lax.rem(x + (NX - q), NX)
                    piece, dev, n2, m2, at2 = buf.at[k, y, h, s], at_x(s), NY, y, at_y
                else:
                    s = lax.rem(y + (NY - q), NY)
                    piece, dev, n2, m2, at2 = buf.at[k, s, h, x], at_y(s), NX, x, at_x
                recv(piece, (s1, r1, (h, q - 1)), dev)
                for j, t, _ in others(n2, m2):
                    send(piece, piece, (s2, r2, (h, q, j)), at2(t))
        to_sibling(buf, y, 0, sc, rc, 0)

    def rest(buf, s2, r2, sc, rc):
        def half0(q):
            yy = lax.rem(y + (NY - q), NY)
            for j in range(NX):
                xx = lax.rem(x + (NX - j), NX)
                recv(buf.at[k, yy, 0, xx], (s2, r2, (0, j, q - 1)), at_y(yy))
            to_sibling(buf, yy, 0, sc, rc, q)

        def half1(j):
            yy = lax.rem(y + (NY - j), NY)
            for q in (1, 3, 2):
                xx = lax.rem(x + (NX - q), NX)
                recv(buf.at[k, yy, 1, xx], (s2, r2, (1, j, q - 1)), at_x(xx))
            to_sibling(buf, yy, 1, sc, rc, j)

        half1(0)
        half0(1)
        half1(1)
        half0(3)
        half1(3)
        half0(2)
        half1(2)

    def all_logits(buf, log, sc, rc):
        def step(n, _):
            q = lax.rem(n, NY)
            yy, kk = lax.rem(y + (NY - q), NY), jnp.where(n < NY, k, 1 - k)

            @pl.when(n >= NY)
            def _():
                for h in range(2):
                    recv(buf.at[1 - k, yy, h], (sc, rc, (h, q)), sibling)

            cc = yy * 2 + kk
            block = pl.ds(pl.multiple_of(cc * COLS, 128), COLS)
            value = buf[kk, yy].reshape(256, COLS)
            log[...] += jnp.dot(value, u[block, :], preferred_element_type=F32)
            if buf is l_buf:
                scale = regain[cc][0:1]
                total = squares[...]
                for i in range(COLS // 128):
                    lanes = slice(i * 128, (i + 1) * 128)
                    plain = value[:, lanes].astype(F32) * scale[:, lanes]
                    total = total + plain * plain
                squares[...] = total
            return 0

        lax.fori_loop(0, 8, step, 0)

    for j, _, (zz, xx) in plane:
        recv(hin.at[slot_of(zz, xx)], (a_s, a_r, (j,)), (zz * NX + xx, c))
    found = hin[...].astype(F32)
    load_tw.wait()
    rows = jnp.concatenate([found[:, :8].reshape(256, 128), found[:, 8:].reshape(256, 128)], axis=1)
    product = jnp.dot(rows.astype(BF16), twp[...], preferred_element_type=F32)
    mapped[...] = product.reshape(2, NX, 32, COLS)
    mapped_b[...] = product.astype(BF16).reshape(2, NX, 32, COLS)
    quarters = [(h, pl.ds(16 * p, 16)) for h in range(2) for p in range(2)]
    for p, (h, part) in enumerate(quarters):
        for j, t, _ in others(NX, x):
            send(mapped_b.at[h, t, part], cx.at[j, h, part], (c_s, c_r, (p, j)), at_x(t))

    def z_sum(src, dst, ss, rs, zz):
        place = lax.rem(zz - z + NZ, NZ) - 1
        return copy(src.at[zz], dst.at[place], ss.at[place], rs.at[place], at_z(zz))

    def z_send(src, dst, ss, rs, zz):
        @pl.when(z != zz)
        def _():
            z_sum(src, dst, ss, rs, zz).start()

    for j, _, s in others(NZ, z):
        recv(f_z.at[s], (fz_s, fz_r, (j,)), at_z(s))
    own_pieces(f_buf, unpack(f_z[...]), f1_s, f1_r, f2_s, f2_r)
    rows_out[...] = rows.T.astype(BF16)
    for p, (h, part) in enumerate(quarters):
        for j, _, s in others(NX, x):
            recv(cx.at[j, h, part], (c_s, c_r, (p, j)), at_x(s))
        total = mapped[h, x, part]
        for j in range(3):
            total = total + cx[j, h, part].astype(F32)
        sx[2 * p : 2 * p + 2] = total.reshape(2, 8, COLS)
        z_send(sx, dz, d_s, d_r, 2 * p)
        z_send(sx, dz, d_s, d_r, 2 * p + 1)
    load_off.wait()
    forward(f_buf, f1_s, f1_r, f2_s, f2_r, fc_s, fc_r)
    base = hid[:, feat].astype(F32) + off[...].reshape(1, COLS) + sx[z]
    gain_part = gains[c]
    for j, _, s in others(NZ, z):
        recv(dz.at[j], (d_s, d_r, (j,)), at_z(s))
        base = base + dz[j]
    l_state[...] = base

    l_pack[...] = pack(base * gain_part)
    for j, t, _ in others(NZ, z):
        send(l_pack, l_z.at[z], (lz_s, lz_r, (j,)), at_z(t))
    l_z[z] = l_pack[...]
    squares[...] = jnp.zeros_like(squares)
    l_log[...] = jnp.zeros_like(l_log)
    f_log[...] = jnp.zeros_like(f_log)
    for j, _, s in others(NZ, z):
        recv(l_z.at[s], (lz_s, lz_r, (j,)), at_z(s))
    own_pieces(l_buf, unpack(l_z[...]), l1_s, l1_r, l2_s, l2_r)
    forward(l_buf, l1_s, l1_r, l2_s, l2_r, lc_s, lc_r)
    rest(f_buf, f2_s, f2_r, fc_s, fc_r)
    load_u.wait()
    all_logits(f_buf, f_log, fc_s, fc_r)
    rest(l_buf, l2_s, l2_r, lc_s, lc_r)
    all_logits(l_buf, l_log, lc_s, lc_r)

    place = lax.broadcasted_iota(jnp.int32, (32, 128), 1)

    def local(i, _):
        part = pl.ds(pl.multiple_of(i * 32, 32), 32)
        mean = jnp.sum(squares[part, :], axis=1, keepdims=True) / D
        inverse = lax.rsqrt(mean + EPSILON)
        inv_cols[part, :] = jnp.broadcast_to(inverse, (32, 128))
        a, b = l_log[part, :] * inverse, f_log[part, :]
        l_log[part, :] = a
        a_peak, b_peak = jnp.max(a, axis=1, keepdims=True), jnp.max(b, axis=1, keepdims=True)
        weight = jnp.exp(b - b_peak)
        found = [
            a_peak, jnp.sum(jnp.exp(a - a_peak), axis=1, keepdims=True), b_peak,
            jnp.sum(weight, axis=1, keepdims=True), jnp.sum(weight * (b - a), axis=1, keepdims=True),
        ]
        tile = jnp.zeros((32, 128), F32)
        for n, v in enumerate(found):
            tile = jnp.where(place == n, jnp.broadcast_to(v, (32, 128)), tile)
        cols[part, :] = tile
        return 0

    lax.fori_loop(0, 8, local, 0)
    st_core[7] = cols[...].T[:8]
    for j, t, _ in group:
        send(st_core.at[7], st_core.at[j], (tc_s, tc_r, (j,)), t)
    for j, _, s in group:
        recv(st_core.at[j], (tc_s, tc_r, (j,)), s)
    found = merge([st_core[j] for j in range(8)])
    for buf, n, me, at, ss, rs in ((st_x, NX, x, at_x, tx_s, tx_r), (st_z, NZ, z, at_z, tz_s, tz_r)):
        buf[n - 1] = found
        for j, t, _ in others(n, me):
            send(buf.at[n - 1], buf.at[j], (ss, rs, (j,)), at(t))
        for j, _, s in others(n, me):
            recv(buf.at[j], (ss, rs, (j,)), at(s))
        found = merge([buf[j] for j in range(n)])
    lens_total = found[0:1] + jnp.log(found[1:2])
    final_total = found[2:3] + jnp.log(found[3:4])
    apart = found[4:5] / found[3:4] + lens_total - final_total
    tall = jnp.concatenate([stack_rows([lens_total, final_total, apart]), jnp.zeros((120, 256), F32)], axis=0)
    cols[...] = tall.T
    mine = pl.ds(pl.multiple_of(half * 128 + x * 32 + quarter * 8, 8), 8)
    div[...] = jnp.broadcast_to(cols[mine, 2:3], (8, 128))

    def slopes(i, _):
        part = pl.ds(pl.multiple_of(i * 32, 32), 32)
        totals = cols[part, :]
        a = l_log[part, :]
        rounded = (jnp.exp(a - totals[:, 0:1]) - jnp.exp(f_log[part, :] - totals[:, 1:2])).astype(BF16)
        grad[part, :] = rounded
        slope = jnp.sum(rounded.astype(F32) * a, axis=1, keepdims=True)
        sl_cols[part, :] = jnp.broadcast_to(slope, (32, 128))
        return 0

    lax.fori_loop(0, 8, slopes, 0)

    def back(yy, kk):
        block = pl.ds(pl.multiple_of((yy * 2 + kk) * COLS, 128), COLS)
        return lax.dot_general(
            grad[...], u[block, :], (((1,), (1,)), ((), ())), preferred_element_type=F32
        ).reshape(2, NX, 32, COLS)

    def slope_send(buf, n, me, at, ss, rs):
        for j, t, _ in others(n, me):
            send(buf.at[n - 1], buf.at[j], (ss, rs, (j,)), at(t))

    def slope_sum(buf, n, me, at, ss, rs):
        total = buf[n - 1]
        for j, _, s in others(n, me):
            recv(buf.at[j], (ss, rs, (j,)), at(s))
            total = total + buf[j]
        return total

    over_y = (sl_y, NY, y, at_y, py_s, py_r)
    over_x = (sl_x, NX, x, at_x, px_s, px_r)
    over_z = (sl_z, NZ, z, at_z, pz_s, pz_r)
    sl_core[0] = sl_cols[...].T[:8]
    send(sl_core.at[0], sl_core.at[1], (pc_s, pc_r, ()), sibling)

    def block_y(i):
        return lax.rem(y + 1 + i, NY)

    def hand_over(i):
        return copy(c_send.at[i], c_recv.at[i], gc_s.at[i], gc_r.at[i], sibling)

    def y_far(p):
        return copy(acc.at[1, 0, pl.ds(2 * p, 2)], fy.at[p], yf_s.at[p], yf_r.at[p], at_y(block_y(2 * p)))

    def y_near(p, part):
        two = pl.ds(2 * part, 2)
        sem = (yn_s.at[p, part], yn_r.at[p, part])
        return copy(acc.at[2 * p, 0, two], ry.at[p, two], *sem, at_y(block_y(2 * p)))

    def beside(i, far):
        return lax.div(i, 2) if far else 1 - lax.div(i, 2)

    def x_at(way):
        return lax.rem(x + 1 + 2 * way, NX)

    def x_far(i):
        way = beside(i, True)
        return copy(acc.at[i, 1, lax.rem(x + 2, NX)], fx.at[i], xf_s.at[i], xf_r.at[i], at_x(x_at(way)))

    def x_near(i):
        way = beside(i, False)
        return copy(acc.at[i, 1, x_at(way)], rx.at[way, i], xn_s.at[i], xn_r.at[i], at_x(x_at(way)))

    def x_sum(i):
        way = beside(i, True)
        return copy(acc.at[i, 1, x_at(way)], rx.at[way, i], xs_s.at[i], xs_r.at[i], at_x(x_at(way)))

    def away(i):
        c_send[i] = back(block_y(i), 1 - k)
        hand_over(i).start()

    def order(i):
        return jnp.where(i < 2, 1 - i, i)

    def home(i, n):
        acc[i] = back(block_y(i), k)
        hand_over(i).wait_recv()
        acc[i] += c_recv[i]

        @pl.when(n == 0)
        def _():
            y_far(0).start()
            y_far(1).start()

        @pl.when(n == 1)
        def _():
            y_near(0, 1).start()

        @pl.when(n == 2)
        def _():
            y_near(1, 0).start()

        x_far(i).start()
        x_near(i).start()

    def both(n, _):
        @pl.when(n < NY)
        def _():
            away(order(n))

        @pl.when(n > 0)
        def _():
            home(order(n - 1), n - 1)

        return 0

    lax.fori_loop(0, NY + 1, both, 0)
    recv(sl_core.at[1], (pc_s, pc_r, ()), sibling)
    sl_y[NY - 1] = sl_core[0] + sl_core[1]
    slope_send(*over_y)
    for p in range(2):
        y_far(p).wait_recv()
        acc[2 * p, 0, 2 * p : 2 * p + 2] += fy[p]
        y_near(p, p).start()
    for i in (1, 0, 2, 3):
        x_far(i).wait_recv()
        acc[i, 1, x_at(beside(i, True))] += fx[i]
        x_sum(i).start()
    for p in range(2):
        for part in range(2):
            y_near(p, part).wait_recv()

    def add0(i, _):
        r0[i] = acc[NY - 1, 0, i] + ry[0, i] + ry[1, i]
        return 0

    lax.fori_loop(0, NX, add0, 0)
    sl_x[NX - 1] = slope_sum(*over_y)
    slope_send(*over_x)
    eights = [pl.ds(8 * q, 8) for q in range(4)]
    for q, part in enumerate(eights):
        for j, t, _ in others(NX, x):
            send(r0.at[t, part], rx0.at[j, part], (g2_s, g2_r, (0, j, q)), at_x(t))

    for i in range(NY):
        x_near(i).wait_recv()
        x_sum(i).wait_recv()
        r1[i] = acc[i, 1, x] + rx[0, i] + rx[1, i]
    for q, part in enumerate(eights):
        for i in range(NY - 1):
            send(r1.at[i, part], ry1.at[i, part], (g2_s, g2_r, (1, i, q)), at_y(block_y(i)))
    sl_z[NZ - 1] = slope_sum(*over_x)
    slope_send(*over_z)
    for q, part in enumerate(eights):
        for j, _, s in others(NX, x):
            recv(rx0.at[j, part], (g2_s, g2_r, (0, j, q)), at_x(s))
        sz[q] = r0[x, part] + rx0[0, part] + rx0[1, part] + rx0[2, part]
        z_send(sz, rz, gz_s, gz_r, q)
        for i in range(NY - 1):
            recv(ry1.at[i, part], (g2_s, g2_r, (1, i, q)), at_y(block_y(i)))
        sz[4 + q] = r1[NY - 1, part] + ry1[0, part] + ry1[1, part] + ry1[2, part]
        z_send(sz, rz, gz_s, gz_r, 4 + q)
    cols[...] = jnp.concatenate([slope_sum(*over_z), jnp.zeros((120, 256), F32)], axis=0).T
    state_grad = sz[z]
    for j, _, s in others(NZ, z):
        recv(rz.at[j], (gz_s, gz_r, (j,)), at_z(s))
        state_grad = state_grad + rz[j]
    inverse = inv_cols[mine, 0:1]
    slope = cols[mine, 0:1] / D
    delta = inverse * (gain_part * state_grad) - l_state[...] * (inverse * inverse * slope)
    sd_z[mine8] = pack(delta)
    own = sd_z.at[mine8]
    for j, t, _ in others(NZ, z):
        send(own, own, (oz_s, oz_r, (j,)), at_z(t))

    def four(hh, xx):
        return sd_z.at[pl.ds(hh * 16 + xx * 4, 4)]

    for near in range(2):
        hh = half if near == 0 else 1 - half
        for i in range(4):
            s = hh * 4 + i

            @pl.when(s != z)
            def _():
                place = lax.rem(z - s + NZ, NZ) - 1
                piece = sd_z.at[slot_of(s, x)]
                copy(piece, piece, oz_s.at[place], oz_r.at[place], at_z(s)).wait_recv()

        for j, t, _ in others(NX, x):
            send(four(hh, x), four(hh, x), (ox_s, ox_r, (near, j)), at_x(t))
    for near in range(2):
        hh = half if near == 0 else 1 - half
        for j, _, s in others(NX, x):
            recv(four(hh, s), (ox_s, ox_r, (near, j)), at_x(s))
    found = sd_z[...].astype(F32)
    sd_out[...] = jnp.concatenate([found[:, :8], found[:, 8:, :384]], axis=2).reshape(256, COLS).astype(BF16)

    for i in range(NY):
        hand_over(i).wait_send()
        x_far(i).wait_send()
        x_near(i).wait_send()
        x_sum(i).wait_send()
    for p in range(2):
        y_far(p).wait_send()
        for part in range(2):
            y_near(p, part).wait_send()
    for _, t, _ in others(NZ, z):
        z_sum(sx, dz, d_s, d_r, t).wait_send()
        z_sum(sz, rz, gz_s, gz_r, t).wait_send()
    for one in unsent:
        one.wait_send()


def finish(rows, delta, div, gt, goff, divergence):
    gt[...] = jnp.dot(rows[...], delta[...], preferred_element_type=F32)[:ROWS]
    goff[...] = jnp.sum(delta[...].astype(F32), axis=0)
    divergence[...] = div[...].T[0]


def on_device(hidden, final_hidden, translator, offset, norm_gain, unembed):
    vm = pltpu.VMEM
    dma = pltpu.SemaphoreType.DMA
    blocks = [
        vm((8, D), BF16), vm((8, D), BF16), vm((COLS,), F32), vm((D,), BF16),
        vm((D, VOC), BF16), vm((32, 16, 128), BF16), vm((32, 16, 128), BF16), vm((256, COLS), BF16),
        vm((2, NX, 32, COLS), F32), vm((2, NX, 32, COLS), BF16), vm((3, 2, 32, COLS), BF16),
        vm((NZ, 8, COLS), F32), vm((7, 8, COLS), F32),
        vm((8, D), F32), vm((16, 512), BF16), vm((NZ, 16, 512), BF16), vm((2, NY, 2, NX, 32, COLS), BF16),
        vm((16, 512), BF16), vm((NZ, 16, 512), BF16), vm((2, NY, 2, NX, 32, COLS), BF16), vm((8, COLS), F32),
        vm((8, 8, COLS), F32), vm((8, 8, COLS), F32), vm((256, 128), F32),
        vm((256, VOC), F32), vm((256, VOC), F32),
        vm((8, 8, 256), F32), vm((NX, 8, 256), F32), vm((NZ, 8, 256), F32),
        vm((2, 8, 256), F32), vm((NY, 8, 256), F32), vm((NX, 8, 256), F32), vm((NZ, 8, 256), F32),
        vm((256, 128), F32), vm((256, 128), F32), vm((256, 128), F32), vm((256, VOC), BF16),
        vm((NY, 2, NX, 32, COLS), F32), vm((NY, 2, NX, 32, COLS), F32), vm((NY, 2, NX, 32, COLS), F32),
        vm((2, 2, 32, COLS), F32), vm((2, NX, 32, COLS), F32), vm((NY, 32, COLS), F32), vm((2, NY, 32, COLS), F32),
        vm((NX, 32, COLS), F32), vm((NY, 32, COLS), F32),
        vm((3, 32, COLS), F32), vm((3, 32, COLS), F32), vm((NZ, 8, COLS), F32), vm((7, 8, COLS), F32),
        vm((32, 16, 512), BF16),
    ]
    pairs = [
        (31,), (4, 3), (7,),
        (7,), (2, 3), (2, 4, 3), (2, 4),
        (7,), (2, 3), (2, 4, 3), (2, 4),
        (7,), (3,), (7,),
        (), (3,), (3,), (7,),
        (4,), (2,), (2, 2), (4,), (4,), (4,), (2, 3, 4), (7,),
        (7,), (2, 3),
    ]
    sems = [dma((6,))]
    for shape in pairs:
        sems += [dma(shape) if shape else dma] * 2
    whole = pl.BlockSpec(memory_space=pltpu.VMEM)
    rows, delta, div = pl.pallas_call(
        kernel,
        out_shape=(
            jax.ShapeDtypeStruct((256, 256), BF16),
            jax.ShapeDtypeStruct((256, COLS), BF16),
            jax.ShapeDtypeStruct((8, 128), F32),
        ),
        in_specs=[pl.BlockSpec(memory_space=pl.ANY)] * 6,
        out_specs=(whole, whole, whole),
        scratch_shapes=blocks + sems,
        compiler_params=pltpu.CompilerParams(
            collective_id=0, has_side_effects=True, vmem_limit_bytes=56 * 2**20
        ),
        name="lens_step",
    )(hidden, final_hidden, translator, offset, norm_gain, unembed)
    return pl.pallas_call(
        finish,
        out_shape=(
            jax.ShapeDtypeStruct((ROWS, COLS), F32),
            jax.ShapeDtypeStruct((COLS,), F32),
            jax.ShapeDtypeStruct((8,), F32),
        ),
        in_specs=[whole] * 3,
        out_specs=(whole, whole, whole),
        name="finish",
    )(rows, delta, div)


def solution(mesh):
    placed = (P("dp", None), P("dp", None), P("dp", "vocab"), P("vocab"), P(), P(None, ("dp", "vocab")))
    return jax.shard_map(
        on_device,
        mesh=mesh,
        in_specs=placed,
        out_specs=(P("dp", "vocab"), P("vocab"), P("dp")),
        check_vma=False,
    )
```
